32 devices in a mesh: groups: 2 (over y), exp: 16 (over z, x, core), base: 1.
Axes of the slice: x: 2, y: 2, z: 4, core: 2. Of those that a mesh axis runs over, the one named last changes fastest.
Arguments:
- tokens: bfloat16 [512, 7168], P(('groups', 'exp', 'base')), parts along dimension 0, may hold values from -6 to 6
- routes: int32 [512, 8], P(('groups', 'exp', 'base')), parts along dimension 0, may hold values from 0 to 15, all different within a row; in each aligned block of 16 rows (0 to 15, 16 to 31, ...) at most 12 rows name the same one
- route_weight: float32 [512, 8], P(('groups', 'exp', 'base')), parts along dimension 0, may hold values from 0.03 to 0.6
- base_index: int32 [16, 8], replicated, may hold values from 0 to 55, as said below
- expert_mask: int32 [16, 16, 8], P('exp'), may hold values 0 or 1
- base_gate: bfloat16 [16, 8, 128, 128], P('base'), may hold values from -0.1875 to 0.1875
- base_up: bfloat16 [16, 8, 128, 128], P('base'), may hold values from -0.1875 to 0.1875
- base_down: bfloat16 [16, 8, 128, 128], P('base'), may hold values from -0.375 to 0.375
- delta_in: bfloat16 [16, 7168, 128], P('exp'), may hold values from -0.0625 to 0.0625
- delta_gate_up: bfloat16 [16, 2, 128, 2048], P('exp', None, None, 'base'), may hold values from -0.5 to 0.5
- delta_down_in: bfloat16 [16, 2048, 128], P('exp', 'base'), may hold values from -0.125 to 0.125
- delta_out: bfloat16 [16, 128, 7168], P('exp'), may hold values from -0.5 to 0.5
Outputs:
- combined: bfloat16 [512, 7168], P(('groups', 'exp', 'base')), parts along dimension 0
The draws below stay inside these ranges and needn't reach their ends.
There are 2 independent parts, one for each index of `groups`. The reference program is written for one: setup_inputs(seed, part) draws one part's arguments, and reference() takes and returns one part's arrays. A program takes and returns all parts, laid end to end along the dimension named above; an argument that names none is the same for every part. Nothing has to cross between parts.
Inputs may be any that keep to these rules, and one draw needn't show every extreme that they name: `routes`: in the rows of one device (aligned blocks of 16 tokens) no expert is named by more than 12 tokens, and the 8 experts of a token differ. `base_index`: the 8 entries of each row differ.
All inputs are finite; a program needn't handle non-finite values. No bound on the sum of `expert_mask` on one device may be relied on, other than what follows from the above.
Results may differ from the reference program's by a relative error of at most 0.0071.
Values may be sent and summed in bfloat16 or wider, within the bound.
A program may use at most 128 MiB of HBM per device.

```python
import math
import jax
import jax.numpy as jnp
import numpy as np
from jax import lax

D = 7168
FF = 2048
TOP = 8
R = 128
KT = 8
TOK_DEV = 16
EXPERTS = 16
TOKENS = 256
FFB = 16
DB = 56
MOST = 12
CAP = 192
N_BASE = 1


def draw_base_index(key, part):
    key = jax.random.fold_in(key, 7)
    row_keys = jax.random.split(key, FFB)

    def one_row(row_key):
        return jax.random.permutation(row_key, DB)[:KT]
    return jax.vmap(one_row)(row_keys).astype(jnp.int32)


def with_ends(drawn, own_key, low, high):
    dims = drawn.shape
    index_at = [jax.random.randint(jax.random.fold_in(own_key, axis), (), 0, dims[axis]) for axis in range(len(dims))]
    drawn = drawn.at[tuple(index_at)].set(low)
    longest = dims.index(max(dims))
    index_at[longest] = (index_at[longest] + 1) % dims[longest]
    return drawn.at[tuple(index_at)].set(high)


def steps_of(stream_key, shape, cuts, smallest, high):
    def one(position, shards_of):
        draws = jax.random.uniform(jax.random.fold_in(jax.random.fold_in(stream_key, 6), position), (shards_of,), jnp.float32, smallest / len(cuts), high / len(cuts))
        return jnp.repeat(jnp.exp(draws), shape[position] // shards_of).reshape((-1,) + (1,) * (len(shape) - position - 1))

    gain = one(*cuts[0])
    for cut in cuts[1:]:
        gain = gain * one(*cut)
    return gain


def shared_out(key, own, number, rows, count, top, bound, skew):
    order = jax.random.permutation(key, count)
    packed, common = portions_of(count, rows * top, bound, skew, True), portions_of(count, rows * top, bound, skew, False)
    places = jnp.arange(count)

    def named(lengths, turn):
        used = int((lengths > 0).sum())
        fixed = max(1, used // 4)
        shifted = fixed + (places - fixed + turn * (used - fixed)) % max(1, count - fixed)
        return jnp.zeros((count,), jnp.int32).at[order[jnp.where(places < fixed, places, shifted)]].set(jnp.asarray(lengths, jnp.int32))

    lengths = jnp.where(number % 4 == 0, named(packed, number // 4), named(common, number - number // 4 - 1))
    mixed = jax.random.permutation(jax.random.fold_in(own, 3), count)
    source_of, receiver = mixed[0:count // 2 * 2:2], mixed[1:count // 2 * 2:2]
    margin = jnp.minimum(lengths[source_of] - 1, bound - lengths[receiver]) // 2
    margin = jnp.where((source_of == order[0]) | (receiver == order[0]) | (lengths[receiver] == 0), 0, jnp.maximum(margin, 0))
    shifted = jax.random.randint(jax.random.fold_in(own, 4), (count // 2,), 0, 1 << 20) % (margin + 1)
    lengths = lengths.at[source_of].add(-shifted).at[receiver].add(shifted)
    items = jnp.searchsorted(jnp.cumsum(lengths), jnp.arange(rows * top), side="right").astype(jnp.int32)
    grid = items.reshape(top, rows).T
    grid = grid[jax.random.permutation(jax.random.fold_in(own, 1), rows)]
    turn = jax.random.randint(jax.random.fold_in(own, 2), (rows, 1), 0, top)
    return jnp.take_along_axis(grid, (jnp.arange(top)[None, :] + turn) % top, axis=1)


def portions_of(count, total, bound, slope, full):
    portions = [(1 << 20) // math.isqrt(standing ** slope) + 1 for standing in range(1, count + 1)]
    largest = bound if full else min(bound, max(-(-total // count), total * portions[0] // sum(portions)))
    least = 1 if total - largest >= count - 1 else 0
    given, spare = [largest] + [least] * (count - 1), total - largest - least * (count - 1)
    while spare > 0:
        movable = [i for i in range(1, count) if given[i] < largest] or [i for i in range(1, count) if given[i] < bound]
        whole, budget = sum([portions[i] for i in movable]), spare
        for i in movable:
            more = min(bound - given[i], max(1, budget * portions[i] // whole), spare)
            given[i] = given[i] + more
            spare = spare - more
    return np.array(given)


def scatter_about(rng, dims, width, most, shards=(), kind=jnp.bfloat16):
    entries = width * jax.random.normal(rng, dims, jnp.float32)
    if shards:
        entries = entries * steps_of(rng, dims, shards, -0.22, 0.18)
    return jnp.clip(entries, -most, most).astype(kind)


def setup_inputs(seed: int = 0, part: int = 0) -> dict:
    keys = jax.random.split(jax.random.key(seed), 13)
    own_keys = jax.random.split(jax.random.fold_in(keys[12], part), 13)
    tokens = scatter_about(own_keys[0], (TOKENS, D), 1.0, 6.0, ((0, 16),))
    routes_keys = jax.random.split(jax.random.fold_in(own_keys[1], 1), TOKENS // TOK_DEV)
    routes_turns = jax.random.permutation(jax.random.fold_in(own_keys[1], 3), TOKENS // TOK_DEV)
    routes = jax.vmap(lambda own, number: shared_out(jax.random.fold_in(own_keys[1], 2), own, number, TOK_DEV, EXPERTS, TOP, MOST, 2))(routes_keys, routes_turns).reshape((TOKENS, TOP))
    route_weight = jnp.clip(jnp.exp(math.log(0.6) - 2.9957323 * jax.random.uniform(own_keys[2], (TOKENS, TOP), jnp.float32) ** steps_of(own_keys[2], (TOKENS, TOP), ((0, 16),), -0.2, 0.2)), 0.03, 0.6)
    base_index = draw_base_index(jax.random.fold_in(keys[12], 71), part)
    expert_mask = with_ends((jax.random.randint(keys[4], (EXPERTS, FFB, KT), 0, 4) < 3).astype(jnp.int32), jax.random.fold_in(keys[4], 1), 0, 1)
    base_gate = scatter_about(keys[5], (FFB, KT, 128, 128), (KT * 128) ** -0.5, 0.1875)
    base_up = scatter_about(keys[6], (FFB, KT, 128, 128), (KT * 128) ** -0.5, 0.1875)
    base_down = scatter_about(keys[7], (FFB, KT, 128, 128), (max(128, FFB * KT * 128 // DB)) ** -0.5, 0.375)
    delta_in = scatter_about(keys[8], (EXPERTS, D, R), D ** -0.5, 0.0625, ((0, 16),))
    delta_gate_up = scatter_about(keys[9], (EXPERTS, 2, R, FF), R ** -0.5, 0.5, ((0, 16),))
    delta_down_in = scatter_about(keys[10], (EXPERTS, FF, R), FF ** -0.5, 0.125, ((0, 16),))
    delta_out = scatter_about(keys[11], (EXPERTS, R, D), R ** -0.5, 0.5, ((0, 16),))
    return dict(tokens=tokens, routes=routes, route_weight=route_weight, base_index=base_index, expert_mask=expert_mask, base_gate=base_gate, base_up=base_up, base_down=base_down, delta_in=delta_in, delta_gate_up=delta_gate_up, delta_down_in=delta_down_in, delta_out=delta_out)


def expert_output(incoming, expert, base_index, expert_mask, base_gate, base_up, base_down, delta_in, delta_gate_up, delta_down_in, delta_out):
    row_count = incoming.shape[0]
    tile_keep = expert_mask[expert].astype(jnp.float32)[:, :, None, None]
    row_cubes = incoming.astype(jnp.float32).reshape(row_count, DB, 128)
    picked = row_cubes[:, base_index]
    pre_gate = jnp.einsum('rfkc,fkch->rfh', picked, base_gate.astype(jnp.float32) * tile_keep).reshape(row_count, FF)
    pre_up = jnp.einsum('rfkc,fkch->rfh', picked, base_up.astype(jnp.float32) * tile_keep).reshape(row_count, FF)
    lowrank = jnp.dot(incoming, delta_in[expert], preferred_element_type=jnp.float32).astype(jnp.bfloat16)
    lifted = jnp.einsum('rq,gqh->grh', lowrank.astype(jnp.float32), delta_gate_up[expert].astype(jnp.float32))
    hidden = (jax.nn.silu(pre_gate + lifted[0]) * (pre_up + lifted[1])).astype(jnp.bfloat16)
    share = FF // N_BASE
    share_blocks = FFB // N_BASE
    total = jnp.zeros((row_count, D), jnp.float32)
    for part_index in range(N_BASE):
        lower = part_index * share
        lower_block = part_index * share_blocks
        hid_part = hidden[:, lower:lower + share]
        weights_part = base_down[lower_block:lower_block + share_blocks].astype(jnp.float32) * tile_keep[lower_block:lower_block + share_blocks]
        pieces = jnp.einsum('rfh,fkhc->rfkc', hid_part.astype(jnp.float32).reshape(row_count, share_blocks, 128), weights_part)
        targets = base_index[lower_block:lower_block + share_blocks].reshape(-1)
        placed = jnp.zeros((row_count, DB, 128), jnp.float32).at[:, targets].add(pieces.reshape(row_count, -1, 128))
        squeezed = jnp.dot(hid_part, delta_down_in[expert][lower:lower + share], preferred_element_type=jnp.float32).astype(jnp.bfloat16)
        partial_value = placed.reshape(row_count, D) + jnp.dot(squeezed, delta_out[expert], preferred_element_type=jnp.float32)
        rounded = lax.optimization_barrier(partial_value.astype(jnp.bfloat16))
        total = total + rounded.astype(jnp.float32)
    return total.astype(jnp.bfloat16)


def reference(tokens, routes, route_weight, base_index, expert_mask, base_gate, base_up, base_down, delta_in, delta_gate_up, delta_down_in, delta_out):
    def per_expert(total_out, expert):
        matches = routes == expert
        routed = jnp.any(matches, axis=1)
        chosen = jnp.nonzero(routed, size=CAP, fill_value=0)[0].astype(jnp.int32)
        filled = jnp.arange(CAP, dtype=jnp.int32) < jnp.sum(routed.astype(jnp.int32))
        weight_row = jnp.sum(jnp.where(matches, route_weight, jnp.zeros_like(route_weight)), axis=1)
        scale = jnp.where(filled, weight_row[chosen], jnp.zeros((CAP,), route_weight.dtype))
        result = expert_output(tokens[chosen], expert, base_index, expert_mask, base_gate, base_up, base_down, delta_in, delta_gate_up, delta_down_in, delta_out)
        total_out = total_out.at[chosen].add(scale[:, None] * result.astype(jnp.float32))
        return total_out, None

    total_out, _ = lax.scan(per_expert, jnp.zeros((TOKENS, D), jnp.float32), jnp.arange(EXPERTS, dtype=jnp.int32))
    return total_out.astype(jnp.bfloat16)
```

```python
import functools

import jax
import jax.numpy as jnp
from jax import lax
from jax.experimental import pallas as pl
from jax.experimental.pallas import tpu as pltpu
from jax.sharding import PartitionSpec as P

LANES = 128


def fused_kernel(
    nz,
    tokens_ref,
    weight_ref,
    meta_ref,
    gate_hbm,
    up_hbm,
    down_hbm,
    first_hbm,
    lift_hbm,
    squeeze_hbm,
    last_hbm,
    out_ref,
    tok,
    columns,
    gate_v,
    up_v,
    down_v,
    first_v,
    lift_v,
    squeeze_v,
    last_v,
    hidden,
    segment,
    part,
    scale,
    from_core,
    from_x,
    from_low,
    from_high,
    to_x,
    to_z,
    acc,
    weight_sem,
    gz_recv,
    gx_recv,
    gc_recv,
    gup_send,
    gdown_send,
    gx_send,
    gc_send,
    rc_recv,
    rx_recv,
    rlow_recv,
    rhigh_recv,
    rc_send,
    rx_send,
    rz_send,
):
    rows, width = tokens_ref.shape
    blocks = width // LANES
    pairs = gate_v.shape[0]
    count_blocks = hidden.shape[0]
    per_block = pairs // count_blocks
    all_rows = tok.shape[0]
    me = lax.axis_index("exp")
    core = lax.rem(me, 2)
    x = lax.rem(me // 2, 2)
    z = me // 4

    def place(pz, px, pc):
        return (pz * 2 + px) * 2 + pc

    core_peer = place(z, x, 1 - core)
    x_peer = place(z, 1 - x, core)
    up_peer = me + 4
    down_peer = me - 4
    has_up = z < nz - 1
    has_down = z > 0

    def fetch(position, source, target):
        return pltpu.make_async_copy(source, target, weight_sem.at[position])

    fetches = [
        fetch(0, first_hbm, first_v),
        fetch(1, gate_hbm, gate_v),
        fetch(2, up_hbm, up_v),
        fetch(3, lift_hbm, lift_v),
        fetch(4, down_hbm, down_v),
        fetch(5, squeeze_hbm, squeeze_v),
        fetch(6, last_hbm, last_v),
    ]

    barrier = pltpu.get_barrier_semaphore()

    def greet(peer):
        pl.semaphore_signal(
            barrier, inc=1, device_id={"exp": peer}, device_id_type=pl.DeviceIdType.MESH
        )

    greet(core_peer)
    greet(x_peer)

    @pl.when(has_up)
    def _():
        greet(up_peer)

    @pl.when(has_down)
    def _():
        greet(down_peer)

    own_rows = pl.ds(pl.multiple_of(me * rows, rows), rows)
    tok[own_rows, :width] = tokens_ref[...]
    weights = weight_ref[...]
    lane = lax.broadcasted_iota(jnp.int32, weights.shape, 1)
    high = weights.astype(jnp.bfloat16)
    rest = weights - high.astype(jnp.float32)
    middle = rest.astype(jnp.bfloat16)
    low_part = rest - middle.astype(jnp.float32)
    experts = 4 * nz
    tok[own_rows, width:] = jnp.where(
        lane < experts,
        high.astype(jnp.float32),
        jnp.where(lane < 2 * experts, middle.astype(jnp.float32), low_part),
    ).astype(jnp.bfloat16)

    degree = 2 + has_up.astype(jnp.int32) + has_down.astype(jnp.int32)
    pl.semaphore_wait(barrier, degree)

    def remote(source, target, send, recv, peer):
        return pltpu.make_async_remote_copy(
            src_ref=source,
            dst_ref=target,
            send_sem=send,
            recv_sem=recv,
            device_id={"exp": peer},
            device_id_type=pl.DeviceIdType.MESH,
        )

    def block_of(pz, px, pc):
        return tok.at[pl.ds(pl.multiple_of(place(pz, px, pc) * rows, rows), rows)]

    def g_up(pz):
        b = block_of(pz, x, core)
        return remote(b, b, gup_send.at[pz], gz_recv.at[pz], up_peer)

    def g_down(pz):
        b = block_of(pz, x, core)
        return remote(b, b, gdown_send.at[pz], gz_recv.at[pz], down_peer)

    def g_x(pz, px):
        b = block_of(pz, px, core)
        return remote(b, b, gx_send.at[pz], gx_recv.at[pz], x_peer)

    def g_core(pz, px, pc):
        b = block_of(pz, px, pc)
        return remote(b, b, gc_send.at[pz, px], gc_recv.at[pz, px], core_peer)

    def both_sides(distance, act):
        @pl.when(z >= distance)
        def _():
            act(z - distance, True)

        @pl.when(z + distance < nz)
        def _():
            act(z + distance, False)

    def spread_x(pz):
        g_x(pz, x).start()
        g_core(pz, x, core).start()

    def pass_on(pz, upward):
        if upward:
            g_up(pz).wait_recv()

            @pl.when(has_up)
            def _():
                g_up(pz).start()
        else:
            g_down(pz).wait_recv()

            @pl.when(has_down)
            def _():
                g_down(pz).start()
        spread_x(pz)

    def cross(pz, upward=True):
        g_x(pz, 1 - x).wait_recv()
        g_core(pz, 1 - x, core).start()

    @pl.when(has_up)
    def _():
        g_up(z).start()

    @pl.when(has_down)
    def _():
        g_down(z).start()

    spread_x(z)
    for one in fetches:
        one.start()
    for distance in range(1, nz):
        both_sides(distance, pass_on)
        if distance == 1:
            cross(z)
        else:
            both_sides(distance - 1, cross)
    both_sides(nz - 1, cross)
    for pz in range(nz):
        for px in range(2):
            g_core(pz, px, 1 - core).wait_recv()
    for pz in range(nz):

        @pl.when(jnp.logical_and(has_up, pz <= z))
        def _():
            g_up(pz).wait_send()

        @pl.when(jnp.logical_and(has_down, pz >= z))
        def _():
            g_down(pz).wait_send()

        g_x(pz, x).wait_send()
        for px in range(2):
            g_core(pz, px, core).wait_send()

    sent = tok[:, width:].astype(jnp.float32)
    lane = lax.broadcasted_iota(jnp.int32, sent.shape, 1)
    mine = jnp.logical_and(lax.rem(lane, experts) == me, lane < 3 * experts)
    column = jnp.sum(jnp.where(mine, sent, 0.0), axis=1, keepdims=True)
    scale[...] = jnp.broadcast_to(column, scale.shape)

    fetches[0].wait()
    depth = 8 * LANES if blocks % 8 == 0 else LANES

    def column_step(d, carry):
        columns[d] = tok[:, pl.ds(pl.multiple_of(d * LANES, LANES), LANES)]
        return carry

    lax.fori_loop(0, blocks, column_step, 0)

    def low_step(step, total):
        at = pl.ds(pl.multiple_of(step * depth, depth), depth)
        return total + jnp.dot(tok[:, at], first_v[at, :], preferred_element_type=jnp.float32)

    low = lax.fori_loop(
        0, width // depth, low_step, jnp.zeros((all_rows, LANES), jnp.float32)
    ).astype(jnp.bfloat16)
    for one in fetches[1:4]:
        one.wait()

    def keep_tile(value):
        some = jnp.full((16, LANES), value.astype(jnp.float32)).astype(jnp.bfloat16)
        return jnp.concatenate([some] * (LANES // 16), axis=0)

    def hidden_step(f, carry):
        left, right = [], []
        for k in range(per_block):
            pair = f * per_block + k
            left.append(columns[meta_ref[0, pair]])
            keep = keep_tile(meta_ref[1, pair])
            right.append(jnp.concatenate([gate_v[pair] * keep, up_v[pair] * keep], axis=1))
        units = pl.ds(pl.multiple_of(f * LANES, LANES), LANES)
        left.append(low)
        right.append(jnp.concatenate([lift_v[0, :, units], lift_v[1, :, units]], axis=1))
        both = jnp.dot(
            jnp.concatenate(left, axis=1),
            jnp.concatenate(right, axis=0),
            preferred_element_type=jnp.float32,
        )
        gate, up = both[:, :LANES], both[:, LANES:]
        hidden[f] = (gate / (1.0 + jnp.exp(-gate)) * up).astype(jnp.bfloat16)
        return carry

    lax.fori_loop(0, count_blocks, hidden_step, 0)
    for one in fetches[4:]:
        one.wait()

    def squeeze_step(f, total):
        at = pl.ds(pl.multiple_of(f * LANES, LANES), LANES)
        return total + jnp.dot(hidden[f], squeeze_v[at, :], preferred_element_type=jnp.float32)

    squeezed = lax.fori_loop(
        0, count_blocks, squeeze_step, jnp.zeros((all_rows, LANES), jnp.float32)
    ).astype(jnp.bfloat16)

    def down_step(step, total):
        pair = meta_ref[2, step]
        tile = down_v[pair] * keep_tile(meta_ref[4, step])
        again = meta_ref[5, step].astype(jnp.float32)
        total = total * again + jnp.dot(
            hidden[meta_ref[3, step]], tile, preferred_element_type=jnp.float32
        )
        segment[step] = total
        return total

    lax.fori_loop(0, pairs, down_step, jnp.zeros((all_rows, LANES), jnp.float32))

    def output_step(d, carry):
        at = pl.ds(pl.multiple_of(d * LANES, LANES), LANES)
        value = jnp.dot(squeezed, last_v[:, at], preferred_element_type=jnp.float32)
        value = value + segment[meta_ref[6, d]] * meta_ref[7, d].astype(jnp.float32)
        value = value.astype(jnp.bfloat16).astype(jnp.float32) * scale[...]
        part[:, at] = value.astype(jnp.bfloat16)
        return carry

    lax.fori_loop(0, blocks, output_step, 0)

    def part_of(pz, px, pc):
        return part.at[pl.ds(pl.multiple_of(place(pz, px, pc) * rows, rows), rows)]

    def r_core(pz, px):
        return remote(
            part_of(pz, px, 1 - core),
            from_core.at[pz, px],
            rc_send.at[pz, px],
            rc_recv.at[pz, px],
            core_peer,
        )

    def r_x(pz):
        return remote(to_x.at[pz], from_x.at[pz], rx_send.at[pz], rx_recv.at[pz], x_peer)

    def r_up(pz):
        return remote(to_z.at[pz], from_low.at[pz], rz_send.at[pz], rlow_recv.at[pz], up_peer)

    def r_down(pz):
        return remote(to_z.at[pz], from_high.at[pz], rz_send.at[pz], rhigh_recv.at[pz], down_peer)

    def wide(value):
        return value.astype(jnp.float32)

    def ordered(act):
        for distance in range(nz - 1, 0, -1):
            both_sides(distance, act)

    def core_start(pz, px):
        r_core(pz, px).start()

    ordered(lambda pz, lower: core_start(pz, 1 - x))
    core_start(z, 1 - x)
    ordered(lambda pz, lower: core_start(pz, x))
    core_start(z, x)

    def x_start(pz, lower=True):
        r_core(pz, 1 - x).wait_recv()
        total = wide(part_of(pz, 1 - x, core)[...]) + wide(from_core[pz, 1 - x])
        to_x[pz] = total.astype(jnp.bfloat16)
        r_x(pz).start()

    ordered(x_start)
    x_start(z)

    def local_sum(pz):
        r_core(pz, x).wait_recv()
        r_x(pz).wait_recv()
        total = wide(part_of(pz, x, core)[...]) + wide(from_core[pz, x])
        return total + wide(from_x[pz])

    def z_step(pz, lower):
        acc[...] = local_sum(pz)
        if lower:

            @pl.when(has_up)
            def _():
                r_down(pz).wait_recv()
                acc[...] += wide(from_high[pz])

            to_z[pz] = acc[...].astype(jnp.bfloat16)
            r_down(pz).start()
        else:

            @pl.when(has_down)
            def _():
                r_up(pz).wait_recv()
                acc[...] += wide(from_low[pz])

            to_z[pz] = acc[...].astype(jnp.bfloat16)
            r_up(pz).start()

    ordered(z_step)
    acc[...] = local_sum(z)

    @pl.when(has_up)
    def _():
        r_down(z).wait_recv()
        acc[...] += wide(from_high[z])

    @pl.when(has_down)
    def _():
        r_up(z).wait_recv()
        acc[...] += wide(from_low[z])

    out_ref[...] = acc[...].astype(jnp.bfloat16)

    for pz in range(nz):
        r_x(pz).wait_send()
        for px in range(2):
            r_core(pz, px).wait_send()

        @pl.when(pz != z)
        def _():
            r_up(pz).wait_send()


def tile_plan(base_index, keep, blocks):
    flat = base_index.reshape(-1)
    pairs = flat.shape[0]
    place = jnp.arange(pairs, dtype=jnp.int32)
    ahead = (flat[:, None] < flat[None, :]) | (
        (flat[:, None] == flat[None, :]) & (place[:, None] < place[None, :])
    )
    rank = jnp.sum(ahead.astype(jnp.int32), axis=0)
    chosen = (rank[:, None] == place[None, :]).astype(jnp.int32)
    keep = keep.reshape(-1)
    order = jnp.sum(chosen * place[:, None], axis=0)
    sorted_keep = jnp.sum(chosen * keep[:, None], axis=0)
    sorted_block = jnp.sum(chosen * flat[:, None], axis=0)
    again = jnp.concatenate(
        [jnp.zeros((1,), jnp.int32), (sorted_block[1:] == sorted_block[:-1]).astype(jnp.int32)]
    )
    block = jnp.arange(blocks, dtype=jnp.int32)
    upto = jnp.sum((flat[:, None] <= block[None, :]).astype(jnp.int32), axis=0)
    used = jnp.any(flat[:, None] == block[None, :], axis=0).astype(jnp.int32)
    size = max(pairs, blocks)

    def row(values):
        return jnp.pad(values, (0, size - values.shape[0]))

    return jnp.stack(
        [
            row(flat),
            row(keep),
            row(order),
            row(order // base_index.shape[1]),
            row(sorted_keep),
            row(again),
            row(jnp.maximum(upto - 1, 0)),
            row(used),
        ]
    )


def per_device_fused(
    tokens,
    routes,
    route_weight,
    base_index,
    expert_mask,
    base_gate,
    base_up,
    base_down,
    delta_in,
    delta_gate_up,
    delta_down_in,
    delta_out,
):
    rows, width = tokens.shape
    experts = lax.axis_size("exp")
    nz = experts // 4
    blocks = width // LANES
    count_blocks, per_block = base_index.shape
    pairs = count_blocks * per_block
    all_rows = rows * experts
    named = routes[:, :, None] == jnp.arange(experts, dtype=jnp.int32)[None, None, :]
    weights = jnp.sum(jnp.where(named, route_weight[:, :, None], 0.0), axis=1)
    weights = jnp.pad(
        jnp.concatenate([weights] * 3, axis=1), ((0, 0), (0, LANES - 3 * experts))
    )
    meta = tile_plan(base_index, expert_mask[0], blocks)
    lift = delta_gate_up[0]
    units = lift.shape[2]
    bf16, f32 = jnp.bfloat16, jnp.float32
    vmem, smem, anywhere = (
        pl.BlockSpec(memory_space=space) for space in (pltpu.VMEM, pltpu.SMEM, pl.ANY)
    )
    dma = pltpu.SemaphoreType.DMA
    return pl.pallas_call(
        functools.partial(fused_kernel, nz),
        out_shape=jax.ShapeDtypeStruct((rows, width), bf16),
        in_specs=[vmem, vmem, smem] + [anywhere] * 7,
        out_specs=vmem,
        scratch_shapes=[
            pltpu.VMEM((all_rows, width + LANES), bf16),
            pltpu.VMEM((blocks, all_rows, LANES), bf16),
            pltpu.VMEM((pairs, LANES, LANES), bf16),
            pltpu.VMEM((pairs, LANES, LANES), bf16),
            pltpu.VMEM((pairs, LANES, LANES), bf16),
            pltpu.VMEM((width, LANES), bf16),
            pltpu.VMEM((2, LANES, units), bf16),
            pltpu.VMEM((units, LANES), bf16),
            pltpu.VMEM((LANES, width), bf16),
            pltpu.VMEM((count_blocks, all_rows, LANES), bf16),
            pltpu.VMEM((pairs, all_rows, LANES), f32),
            pltpu.VMEM((all_rows, width), bf16),
            pltpu.VMEM((all_rows, LANES), f32),
            pltpu.VMEM((nz, 2, rows, width), bf16),
            pltpu.VMEM((nz, rows, width), bf16),
            pltpu.VMEM((nz, rows, width), bf16),
            pltpu.VMEM((nz, rows, width), bf16),
            pltpu.VMEM((nz, rows, width), bf16),
            pltpu.VMEM((nz, rows, width), bf16),
            pltpu.VMEM((rows, width), f32),
            dma((7,)),
            dma((nz,)),
            dma((nz,)),
            dma((nz, 2)),
            dma((nz,)),
            dma((nz,)),
            dma((nz,)),
            dma((nz, 2)),
            dma((nz, 2)),
            dma((nz,)),
            dma((nz,)),
            dma((nz,)),
            dma((nz, 2)),
            dma((nz,)),
            dma((nz,)),
        ],
        compiler_params=pltpu.CompilerParams(
            collective_id=0, has_side_effects=True, vmem_limit_bytes=60 << 20
        ),
        name="expert_layer",
    )(
        tokens,
        weights,
        meta,
        base_gate.reshape(pairs, LANES, LANES),
        base_up.reshape(pairs, LANES, LANES),
        base_down.reshape(pairs, LANES, LANES),
        delta_in[0],
        lift,
        delta_down_in[0],
        delta_out[0],
    )


def place_rows(route_block, experts, most_rows, copies, copy_index):
    flat_routes = route_block.reshape(-1)
    onehot = (flat_routes[:, None] == jnp.arange(experts, dtype=jnp.int32)[None, :]).astype(
        jnp.int32
    )
    before = jnp.cumsum(onehot, axis=0) - onehot
    slot_index = jnp.sum(before * onehot, axis=1)
    return (flat_routes * copies + copy_index) * most_rows + slot_index


def spread_matrix(targets, slot_count, choose):
    matches = targets[None, :] == jnp.arange(slot_count, dtype=jnp.int32)[:, None]
    return jnp.any(matches.reshape(slot_count, -1, choose), axis=2).astype(jnp.bfloat16)


def hidden_units(incoming, index_part, keep_part, gate_tiles, up_tiles, delta_first, lift):
    row_count, model_width = incoming.shape
    blocks = model_width // 128
    count_blocks, per_block = index_part.shape
    picked = jnp.take(incoming.reshape(row_count, blocks, 128), index_part.reshape(-1), axis=1)
    picked = picked.reshape(row_count, count_blocks, per_block, 128)
    tile_keep = keep_part.astype(jnp.bfloat16)[:, :, None, None]
    pre_gate = jnp.einsum(
        "rfkc,fkch->rfh", picked, gate_tiles * tile_keep, preferred_element_type=jnp.float32
    ).reshape(row_count, -1)
    pre_up = jnp.einsum(
        "rfkc,fkch->rfh", picked, up_tiles * tile_keep, preferred_element_type=jnp.float32
    ).reshape(row_count, -1)
    lowrank = jnp.dot(incoming, delta_first, preferred_element_type=jnp.float32).astype(
        jnp.bfloat16
    )
    lifted = jnp.einsum("rq,gqh->grh", lowrank, lift, preferred_element_type=jnp.float32)
    return (jax.nn.silu(pre_gate + lifted[0]) * (pre_up + lifted[1])).astype(jnp.bfloat16)


def share_partial(hidden_part, index_part, keep_part, down_tiles, squeeze, delta_last):
    row_count = hidden_part.shape[0]
    count_blocks = down_tiles.shape[0]
    model_width = delta_last.shape[1]
    tile_keep = keep_part.astype(jnp.bfloat16)[:, :, None, None]
    pieces = jnp.einsum(
        "rfh,fkhc->rfkc",
        hidden_part.reshape(row_count, count_blocks, 128),
        down_tiles * tile_keep,
        preferred_element_type=jnp.float32,
    )
    placed = (
        jnp.zeros((row_count, model_width // 128, 128), jnp.float32)
        .at[:, index_part.reshape(-1)]
        .add(pieces.reshape(row_count, -1, 128))
    )
    squeezed = jnp.dot(hidden_part, squeeze, preferred_element_type=jnp.float32).astype(
        jnp.bfloat16
    )
    return placed.reshape(row_count, model_width) + jnp.dot(
        squeezed, delta_last, preferred_element_type=jnp.float32
    )


def per_device(
    tokens,
    routes,
    route_weight,
    base_index,
    expert_mask,
    base_gate,
    base_up,
    base_down,
    delta_in,
    delta_gate_up,
    delta_down_in,
    delta_out,
):
    tok_count, model_width = tokens.shape
    choose = routes.shape[1]
    exp_size = lax.axis_size("exp")
    base_size = lax.axis_size("base")
    half_blocks = base_gate.shape[0]
    most_rows = min(tok_count, max(2, (tok_count * choose + exp_size - 1) // exp_size * 3 // 2))
    own_targets = place_rows(routes, exp_size, most_rows, 1, 0)
    offset = lax.axis_index("base") * half_blocks
    my_index = lax.dynamic_slice_in_dim(base_index, offset, half_blocks, 0)
    my_keep = lax.dynamic_slice_in_dim(expert_mask[0], offset, half_blocks, 0)
    pair_tokens, pair_routes = (
        lax.all_gather(tokens, "base", axis=0, tiled=True),
        lax.all_gather(routes.astype(jnp.bfloat16), "base", axis=0, tiled=True),
    )
    pair_routes = pair_routes.astype(jnp.int32)
    targets = jnp.concatenate(
        [
            place_rows(
                pair_routes[copy_index * tok_count : (copy_index + 1) * tok_count],
                exp_size,
                most_rows,
                base_size,
                copy_index,
            )
            for copy_index in range(base_size)
        ]
    )
    spread = spread_matrix(targets, exp_size * base_size * most_rows, choose)
    outgoing = jnp.dot(spread, pair_tokens, preferred_element_type=jnp.float32).astype(jnp.bfloat16)
    outgoing = outgoing.reshape(exp_size, base_size * most_rows, model_width)
    arrived = lax.all_to_all(outgoing, "exp", split_axis=0, concat_axis=0, tiled=True)
    incoming = arrived.reshape(-1, model_width)
    hidden = hidden_units(
        incoming, my_index, my_keep, base_gate, base_up, delta_in[0], delta_gate_up[0]
    )
    partial_value = share_partial(
        hidden, my_index, my_keep, base_down, delta_down_in[0], delta_out[0]
    )
    summed = lax.psum_scatter(
        partial_value.reshape(exp_size, base_size, most_rows, model_width).astype(jnp.bfloat16),
        "base",
        scatter_dimension=1,
        tiled=True,
    )
    results = summed.reshape(exp_size, most_rows, model_width)
    returned = lax.all_to_all(results, "exp", split_axis=0, concat_axis=0, tiled=True).reshape(
        exp_size * most_rows, model_width
    )
    gathered = returned[own_targets.reshape(tok_count, choose)]
    combined = jnp.sum(route_weight[:, :, None] * gathered.astype(jnp.float32), axis=1)
    return combined.astype(jnp.bfloat16)


def solution(mesh):
    small = mesh.shape["base"] == 1 and mesh.shape["exp"] == 16
    return jax.shard_map(
        per_device_fused if small else per_device,
        mesh=mesh,
        in_specs=(
            P(("groups", "exp", "base"), None),
            P(("groups", "exp", "base"), None),
            P(("groups", "exp", "base"), None),
            P(),
            P("exp", None, None),
            P("base", None, None, None),
            P("base", None, None, None),
            P("base", None, None, None),
            P("exp", None, None),
            P("exp", None, None, "base"),
            P("exp", "base", None),
            P("exp", None, None),
        ),
        out_specs=P(("groups", "exp", "base"), None),
        check_vma=False,
    )
```

```python
import functools

import jax
import jax.numpy as jnp
from jax import lax
from jax.experimental import pallas as pl
from jax.experimental.pallas import tpu as pltpu
from jax.sharding import PartitionSpec as P

LANES = 128


def fused_kernel(
    nz,
    tokens_ref,
    weight_ref,
    meta_ref,
    gate_hbm,
    up_hbm,
    down_hbm,
    first_hbm,
    lift_hbm,
    squeeze_hbm,
    last_hbm,
    out_ref,
    tok,
    columns,
    gate_v,
    up_v,
    down_v,
    first_v,
    lift_v,
    squeeze_v,
    last_v,
    hidden,
    segment,
    part,
    scale,
    from_core,
    from_x,
    from_low,
    from_high,
    to_x,
    to_z,
    acc,
    weight_sem,
    gz_recv,
    gx_recv,
    gc_recv,
    gup_send,
    gdown_send,
    gx_send,
    gc_send,
    rc_recv,
    rx_recv,
    rlow_recv,
    rhigh_recv,
    rc_send,
    rx_send,
    rz_send,
):
    rows, width = tokens_ref.shape
    blocks = width // LANES
    pairs = gate_v.shape[0]
    count_blocks = hidden.shape[0]
    per_block = pairs // count_blocks
    all_rows = tok.shape[0]
    me = lax.axis_index("exp")
    core = lax.rem(me, 2)
    x = lax.rem(me // 2, 2)
    z = me // 4

    def place(pz, px, pc):
        return (pz * 2 + px) * 2 + pc

    core_peer = place(z, x, 1 - core)
    x_peer = place(z, 1 - x, core)
    up_peer = me + 4
    down_peer = me - 4
    has_up = z < nz - 1
    has_down = z > 0

    def fetch(position, source, target):
        return pltpu.make_async_copy(source, target, weight_sem.at[position])

    fetches = [
        fetch(0, first_hbm, first_v),
        fetch(1, gate_hbm, gate_v),
        fetch(2, up_hbm, up_v),
        fetch(3, lift_hbm, lift_v),
        fetch(4, down_hbm, down_v),
        fetch(5, squeeze_hbm, squeeze_v),
        fetch(6, last_hbm, last_v),
    ]

    barrier = pltpu.get_barrier_semaphore()

    def greet(peer):
        pl.semaphore_signal(
            barrier, inc=1, device_id={"exp": peer}, device_id_type=pl.DeviceIdType.MESH
        )

    greet(core_peer)
    greet(x_peer)

    @pl.when(has_up)
    def _():
        greet(up_peer)

    @pl.when(has_down)
    def _():
        greet(down_peer)

    own_rows = pl.ds(pl.multiple_of(me * rows, rows), rows)
    tok[own_rows, :width] = tokens_ref[...]
    weights = weight_ref[...]
    lane = lax.broadcasted_iota(jnp.int32, weights.shape, 1)
    high = weights.astype(jnp.bfloat16)
    rest = weights - high.astype(jnp.float32)
    middle = rest.astype(jnp.bfloat16)
    low_part = rest - middle.astype(jnp.float32)
    experts = 4 * nz
    tok[own_rows, width:] = jnp.where(
        lane < experts,
        high.astype(jnp.float32),
        jnp.where(lane < 2 * experts, middle.astype(jnp.float32), low_part),
    ).astype(jnp.bfloat16)

    degree = 2 + has_up.astype(jnp.int32) + has_down.astype(jnp.int32)
    pl.semaphore_wait(barrier, degree)

    def remote(source, target, send, recv, peer):
        return pltpu.make_async_remote_copy(
            src_ref=source,
            dst_ref=target,
            send_sem=send,
            recv_sem=recv,
            device_id={"exp": peer},
            device_id_type=pl.DeviceIdType.MESH,
        )

    def block_of(pz, px, pc):
        return tok.at[pl.ds(pl.multiple_of(place(pz, px, pc) * rows, rows), rows)]

    def g_up(pz):
        b = block_of(pz, x, core)
        return remote(b, b, gup_send.at[pz], gz_recv.at[pz], up_peer)

    def g_down(pz):
        b = block_of(pz, x, core)
        return remote(b, b, gdown_send.at[pz], gz_recv.at[pz], down_peer)

    def g_x(pz, px):
        b = block_of(pz, px, core)
        return remote(b, b, gx_send.at[pz], gx_recv.at[pz], x_peer)

    def g_core(pz, px, pc):
        b = block_of(pz, px, pc)
        return remote(b, b, gc_send.at[pz, px], gc_recv.at[pz, px], core_peer)

    def both_sides(distance, act):
        @pl.when(z >= distance)
        def _():
            act(z - distance, True)

        @pl.when(z + distance < nz)
        def _():
            act(z + distance, False)

    def spread_x(pz):
        g_x(pz, x).start()
        g_core(pz, x, core).start()

    def pass_on(pz, upward):
        if upward:
            g_up(pz).wait_recv()

            @pl.when(has_up)
            def _():
                g_up(pz).start()
        else:
            g_down(pz).wait_recv()

            @pl.when(has_down)
            def _():
                g_down(pz).start()
        spread_x(pz)

    def cross(pz, upward=True):
        g_x(pz, 1 - x).wait_recv()
        g_core(pz, 1 - x, core).start()

    @pl.when(has_up)
    def _():
        g_up(z).start()

    @pl.when(has_down)
    def _():
        g_down(z).start()

    spread_x(z)
    for one in fetches:
        one.start()
    half_rows = all_rows // 2
    own_half = z // (nz // 2)
    other_half = 1 - own_half

    def half_at(half):
        return pl.ds(pl.multiple_of(half * half_rows, half_rows), half_rows)

    def core_arrived(half):
        for step in range(nz // 2):
            for px in range(2):
                g_core(half * (nz // 2) + step, px, 1 - core).wait_recv()

    depth = 8 * LANES if blocks % 8 == 0 else LANES

    def keep_tile(value):
        some = jnp.full((16, LANES), value.astype(jnp.float32)).astype(jnp.bfloat16)
        return jnp.concatenate([some] * (LANES // 16), axis=0)

    def compute_hidden(half):
        at_rows = half_at(half)
        sent = tok[at_rows, width:].astype(jnp.float32)
        lane = lax.broadcasted_iota(jnp.int32, sent.shape, 1)
        mine = jnp.logical_and(lax.rem(lane, experts) == me, lane < 3 * experts)
        column = jnp.sum(jnp.where(mine, sent, 0.0), axis=1, keepdims=True)
        scale[...] = jnp.broadcast_to(column, scale.shape)

        def column_step(d, carry):
            columns[d] = tok[at_rows, pl.ds(pl.multiple_of(d * LANES, LANES), LANES)]
            return carry

        lax.fori_loop(0, blocks, column_step, 0, unroll=4)

        def low_step(step, total):
            at = pl.ds(pl.multiple_of(step * depth, depth), depth)
            return total + jnp.dot(
                tok[at_rows, at], first_v[at, :], preferred_element_type=jnp.float32
            )

        low = lax.fori_loop(
            0, width // depth, low_step, jnp.zeros((half_rows, LANES), jnp.float32)
        ).astype(jnp.bfloat16)

        def hidden_step(f, carry):
            left, right = [], []
            for k in range(per_block):
                pair = f * per_block + k
                left.append(columns[meta_ref[0, pair]])
                keep = keep_tile(meta_ref[1, pair])
                right.append(jnp.concatenate([gate_v[pair] * keep, up_v[pair] * keep], axis=1))
            units = pl.ds(pl.multiple_of(f * LANES, LANES), LANES)
            left.append(low)
            right.append(jnp.concatenate([lift_v[0, :, units], lift_v[1, :, units]], axis=1))
            both = jnp.dot(
                jnp.concatenate(left, axis=1),
                jnp.concatenate(right, axis=0),
                preferred_element_type=jnp.float32,
            )
            gate, up = both[:, :LANES], both[:, LANES:]
            hidden[f] = (gate / (1.0 + jnp.exp(-gate)) * up).astype(jnp.bfloat16)
            return carry

        lax.fori_loop(0, count_blocks, hidden_step, 0, unroll=2)

    def compute_part(half):
        at_rows = half_at(half)

        def squeeze_step(f, total):
            at = pl.ds(pl.multiple_of(f * LANES, LANES), LANES)
            return total + jnp.dot(hidden[f], squeeze_v[at, :], preferred_element_type=jnp.float32)

        squeezed = lax.fori_loop(
            0, count_blocks, squeeze_step, jnp.zeros((half_rows, LANES), jnp.float32), unroll=8
        ).astype(jnp.bfloat16)

        def down_step(step, total):
            pair = meta_ref[2, step]
            tile = down_v[pair] * keep_tile(meta_ref[4, step])
            again = meta_ref[5, step].astype(jnp.float32)
            total = total * again + jnp.dot(
                hidden[meta_ref[3, step]], tile, preferred_element_type=jnp.float32
            )
            segment[step] = total
            return total

        lax.fori_loop(
            0, pairs, down_step, jnp.zeros((half_rows, LANES), jnp.float32), unroll=8
        )

        def output_step(d, carry):
            at = pl.ds(pl.multiple_of(d * LANES, LANES), LANES)
            value = jnp.dot(squeezed, last_v[:, at], preferred_element_type=jnp.float32)
            value = value + segment[meta_ref[6, d]] * meta_ref[7, d].astype(jnp.float32)
            value = value.astype(jnp.bfloat16).astype(jnp.float32) * scale[...]
            part[at_rows, at] = value.astype(jnp.bfloat16)
            return carry

        lax.fori_loop(0, blocks, output_step, 0, unroll=4)

    for distance in range(1, nz - 1):
        both_sides(distance, pass_on)
        if distance == 1:
            cross(z)
        else:
            both_sides(distance - 1, cross)
    core_arrived(own_half)
    for one in fetches[:4]:
        one.wait()
    compute_hidden(own_half)
    both_sides(nz - 1, pass_on)
    both_sides(nz - 2, cross)
    for one in fetches[4:]:
        one.wait()
    compute_part(own_half)
    both_sides(nz - 1, cross)
    core_arrived(other_half)

    def part_of(pz, px, pc):
        return part.at[pl.ds(pl.multiple_of(place(pz, px, pc) * rows, rows), rows)]

    def r_core(pz, px):
        return remote(
            part_of(pz, px, 1 - core),
            from_core.at[pz, px],
            rc_send.at[pz, px],
            rc_recv.at[pz, px],
            core_peer,
        )

    def r_x(pz):
        return remote(to_x.at[pz], from_x.at[pz], rx_send.at[pz], rx_recv.at[pz], x_peer)

    def r_up(pz):
        return remote(to_z.at[pz], from_low.at[pz], rz_send.at[pz], rlow_recv.at[pz], up_peer)

    def r_down(pz):
        return remote(to_z.at[pz], from_high.at[pz], rz_send.at[pz], rhigh_recv.at[pz], down_peer)

    def wide(value):
        return value.astype(jnp.float32)

    def ordered(act):
        for distance in range(nz - 1, 0, -1):
            both_sides(distance, act)

    def core_start(pz, px):
        r_core(pz, px).start()

    mate = own_half * nz + nz // 2 - 1 - z

    def other_side(act):
        near = jnp.where(own_half == 0, nz // 2, nz // 2 - 1)
        toward = 1 - 2 * own_half
        for step in range(nz // 2 - 1, -1, -1):
            act(near + toward * step)

    core_start(mate, 1 - x)
    core_start(z, 1 - x)
    core_start(mate, x)
    core_start(z, x)
    compute_hidden(other_half)

    def x_start(pz):
        r_core(pz, 1 - x).wait_recv()
        total = wide(part_of(pz, 1 - x, core)[...]) + wide(from_core[pz, 1 - x])
        to_x[pz] = total.astype(jnp.bfloat16)
        r_x(pz).start()

    x_start(mate)
    x_start(z)
    compute_part(other_half)
    other_side(lambda pz: core_start(pz, 1 - x))
    other_side(lambda pz: core_start(pz, x))
    other_side(x_start)

    def local_sum(pz):
        r_core(pz, x).wait_recv()
        r_x(pz).wait_recv()
        total = wide(part_of(pz, x, core)[...]) + wide(from_core[pz, x])
        return total + wide(from_x[pz])

    def z_step(pz, lower):
        acc[...] = local_sum(pz)
        if lower:

            @pl.when(has_up)
            def _():
                r_down(pz).wait_recv()
                acc[...] += wide(from_high[pz])

            to_z[pz] = acc[...].astype(jnp.bfloat16)
            r_down(pz).start()
        else:

            @pl.when(has_down)
            def _():
                r_up(pz).wait_recv()
                acc[...] += wide(from_low[pz])

            to_z[pz] = acc[...].astype(jnp.bfloat16)
            r_up(pz).start()

    ordered(z_step)
    acc[...] = local_sum(z)

    @pl.when(has_up)
    def _():
        r_down(z).wait_recv()
        acc[...] += wide(from_high[z])

    @pl.when(has_down)
    def _():
        r_up(z).wait_recv()
        acc[...] += wide(from_low[z])

    out_ref[...] = acc[...].astype(jnp.bfloat16)

    for pz in range(nz):
        r_x(pz).wait_send()
        for px in range(2):
            r_core(pz, px).wait_send()

        @pl.when(pz != z)
        def _():
            r_up(pz).wait_send()

    for pz in range(nz):

        @pl.when(jnp.logical_and(has_up, pz <= z))
        def _():
            g_up(pz).wait_send()

        @pl.when(jnp.logical_and(has_down, pz >= z))
        def _():
            g_down(pz).wait_send()

        g_x(pz, x).wait_send()
        for px in range(2):
            g_core(pz, px, core).wait_send()


def tile_plan(base_index, keep, blocks):
    flat = base_index.reshape(-1)
    pairs = flat.shape[0]
    place = jnp.arange(pairs, dtype=jnp.int32)
    ahead = (flat[:, None] < flat[None, :]) | (
        (flat[:, None] == flat[None, :]) & (place[:, None] < place[None, :])
    )
    rank = jnp.sum(ahead.astype(jnp.int32), axis=0)
    chosen = (rank[:, None] == place[None, :]).astype(jnp.int32)
    keep = keep.reshape(-1)
    order = jnp.sum(chosen * place[:, None], axis=0)
    sorted_keep = jnp.sum(chosen * keep[:, None], axis=0)
    sorted_block = jnp.sum(chosen * flat[:, None], axis=0)
    again = jnp.concatenate(
        [jnp.zeros((1,), jnp.int32), (sorted_block[1:] == sorted_block[:-1]).astype(jnp.int32)]
    )
    block = jnp.arange(blocks, dtype=jnp.int32)
    upto = jnp.sum((flat[:, None] <= block[None, :]).astype(jnp.int32), axis=0)
    used = jnp.any(flat[:, None] == block[None, :], axis=0).astype(jnp.int32)
    size = max(pairs, blocks)

    def row(values):
        return jnp.pad(values, (0, size - values.shape[0]))

    return jnp.stack(
        [
            row(flat),
            row(keep),
            row(order),
            row(order // base_index.shape[1]),
            row(sorted_keep),
            row(again),
            row(jnp.maximum(upto - 1, 0)),
            row(used),
        ]
    )


def per_device_fused(
    tokens,
    routes,
    route_weight,
    base_index,
    expert_mask,
    base_gate,
    base_up,
    base_down,
    delta_in,
    delta_gate_up,
    delta_down_in,
    delta_out,
):
    rows, width = tokens.shape
    experts = lax.axis_size("exp")
    nz = experts // 4
    blocks = width // LANES
    count_blocks, per_block = base_index.shape
    pairs = count_blocks * per_block
    all_rows = rows * experts
    named = routes[:, :, None] == jnp.arange(experts, dtype=jnp.int32)[None, None, :]
    weights = jnp.sum(jnp.where(named, route_weight[:, :, None], 0.0), axis=1)
    weights = jnp.pad(
        jnp.concatenate([weights] * 3, axis=1), ((0, 0), (0, LANES - 3 * experts))
    )
    meta = tile_plan(base_index, expert_mask[0], blocks)
    lift = delta_gate_up[0]
    units = lift.shape[2]
    bf16, f32 = jnp.bfloat16, jnp.float32
    vmem, smem, anywhere = (
        pl.BlockSpec(memory_space=space) for space in (pltpu.VMEM, pltpu.SMEM, pl.ANY)
    )
    dma = pltpu.SemaphoreType.DMA
    return pl.pallas_call(
        functools.partial(fused_kernel, nz),
        out_shape=jax.ShapeDtypeStruct((rows, width), bf16),
        in_specs=[vmem, vmem, smem] + [anywhere] * 7,
        out_specs=vmem,
        scratch_shapes=[
            pltpu.VMEM((all_rows, width + LANES), bf16),
            pltpu.VMEM((blocks, all_rows // 2, LANES), bf16),
            pltpu.VMEM((pairs, LANES, LANES), bf16),
            pltpu.VMEM((pairs, LANES, LANES), bf16),
            pltpu.VMEM((pairs, LANES, LANES), bf16),
            pltpu.VMEM((width, LANES), bf16),
            pltpu.VMEM((2, LANES, units), bf16),
            pltpu.VMEM((units, LANES), bf16),
            pltpu.VMEM((LANES, width), bf16),
            pltpu.VMEM((count_blocks, all_rows // 2, LANES), bf16),
            pltpu.VMEM((pairs, all_rows // 2, LANES), f32),
            pltpu.VMEM((all_rows, width), bf16),
            pltpu.VMEM((all_rows // 2, LANES), f32),
            pltpu.VMEM((nz, 2, rows, width), bf16),
            pltpu.VMEM((nz, rows, width), bf16),
            pltpu.VMEM((nz, rows, width), bf16),
            pltpu.VMEM((nz, rows, width), bf16),
            pltpu.VMEM((nz, rows, width), bf16),
            pltpu.VMEM((nz, rows, width), bf16),
            pltpu.VMEM((rows, width), f32),
            dma((7,)),
            dma((nz,)),
            dma((nz,)),
            dma((nz, 2)),
            dma((nz,)),
            dma((nz,)),
            dma((nz,)),
            dma((nz, 2)),
            dma((nz, 2)),
            dma((nz,)),
            dma((nz,)),
            dma((nz,)),
            dma((nz, 2)),
            dma((nz,)),
            dma((nz,)),
        ],
        compiler_params=pltpu.CompilerParams(
            collective_id=0, has_side_effects=True, vmem_limit_bytes=60 << 20
        ),
        name="expert_layer",
    )(
        tokens,
        weights,
        meta,
        base_gate.reshape(pairs, LANES, LANES),
        base_up.reshape(pairs, LANES, LANES),
        base_down.reshape(pairs, LANES, LANES),
        delta_in[0],
        lift,
        delta_down_in[0],
        delta_out[0],
    )


def place_rows(route_block, experts, most_rows, copies, copy_index):
    flat_routes = route_block.reshape(-1)
    onehot = (flat_routes[:, None] == jnp.arange(experts, dtype=jnp.int32)[None, :]).astype(
        jnp.int32
    )
    before = jnp.cumsum(onehot, axis=0) - onehot
    slot_index = jnp.sum(before * onehot, axis=1)
    return (flat_routes * copies + copy_index) * most_rows + slot_index


def spread_matrix(targets, slot_count, choose):
    matches = targets[None, :] == jnp.arange(slot_count, dtype=jnp.int32)[:, None]
    return jnp.any(matches.reshape(slot_count, -1, choose), axis=2).astype(jnp.bfloat16)


def hidden_units(incoming, index_part, keep_part, gate_tiles, up_tiles, delta_first, lift):
    row_count, model_width = incoming.shape
    blocks = model_width // 128
    count_blocks, per_block = index_part.shape
    picked = jnp.take(incoming.reshape(row_count, blocks, 128), index_part.reshape(-1), axis=1)
    picked = picked.reshape(row_count, count_blocks, per_block, 128)
    tile_keep = keep_part.astype(jnp.bfloat16)[:, :, None, None]
    pre_gate = jnp.einsum(
        "rfkc,fkch->rfh", picked, gate_tiles * tile_keep, preferred_element_type=jnp.float32
    ).reshape(row_count, -1)
    pre_up = jnp.einsum(
        "rfkc,fkch->rfh", picked, up_tiles * tile_keep, preferred_element_type=jnp.float32
    ).reshape(row_count, -1)
    lowrank = jnp.dot(incoming, delta_first, preferred_element_type=jnp.float32).astype(
        jnp.bfloat16
    )
    lifted = jnp.einsum("rq,gqh->grh", lowrank, lift, preferred_element_type=jnp.float32)
    return (jax.nn.silu(pre_gate + lifted[0]) * (pre_up + lifted[1])).astype(jnp.bfloat16)


def share_partial(hidden_part, index_part, keep_part, down_tiles, squeeze, delta_last):
    row_count = hidden_part.shape[0]
    count_blocks = down_tiles.shape[0]
    model_width = delta_last.shape[1]
    tile_keep = keep_part.astype(jnp.bfloat16)[:, :, None, None]
    pieces = jnp.einsum(
        "rfh,fkhc->rfkc",
        hidden_part.reshape(row_count, count_blocks, 128),
        down_tiles * tile_keep,
        preferred_element_type=jnp.float32,
    )
    placed = (
        jnp.zeros((row_count, model_width // 128, 128), jnp.float32)
        .at[:, index_part.reshape(-1)]
        .add(pieces.reshape(row_count, -1, 128))
    )
    squeezed = jnp.dot(hidden_part, squeeze, preferred_element_type=jnp.float32).astype(
        jnp.bfloat16
    )
    return placed.reshape(row_count, model_width) + jnp.dot(
        squeezed, delta_last, preferred_element_type=jnp.float32
    )


def per_device(
    tokens,
    routes,
    route_weight,
    base_index,
    expert_mask,
    base_gate,
    base_up,
    base_down,
    delta_in,
    delta_gate_up,
    delta_down_in,
    delta_out,
):
    tok_count, model_width = tokens.shape
    choose = routes.shape[1]
    exp_size = lax.axis_size("exp")
    base_size = lax.axis_size("base")
    half_blocks = base_gate.shape[0]
    most_rows = min(tok_count, max(2, (tok_count * choose + exp_size - 1) // exp_size * 3 // 2))
    own_targets = place_rows(routes, exp_size, most_rows, 1, 0)
    offset = lax.axis_index("base") * half_blocks
    my_index = lax.dynamic_slice_in_dim(base_index, offset, half_blocks, 0)
    my_keep = lax.dynamic_slice_in_dim(expert_mask[0], offset, half_blocks, 0)
    pair_tokens, pair_routes = (
        lax.all_gather(tokens, "base", axis=0, tiled=True),
        lax.all_gather(routes.astype(jnp.bfloat16), "base", axis=0, tiled=True),
    )
    pair_routes = pair_routes.astype(jnp.int32)
    targets = jnp.concatenate(
        [
            place_rows(
                pair_routes[copy_index * tok_count : (copy_index + 1) * tok_count],
                exp_size,
                most_rows,
                base_size,
                copy_index,
            )
            for copy_index in range(base_size)
        ]
    )
    spread = spread_matrix(targets, exp_size * base_size * most_rows, choose)
    outgoing = jnp.dot(spread, pair_tokens, preferred_element_type=jnp.float32).astype(jnp.bfloat16)
    outgoing = outgoing.reshape(exp_size, base_size * most_rows, model_width)
    arrived = lax.all_to_all(outgoing, "exp", split_axis=0, concat_axis=0, tiled=True)
    incoming = arrived.reshape(-1, model_width)
    hidden = hidden_units(
        incoming, my_index, my_keep, base_gate, base_up, delta_in[0], delta_gate_up[0]
    )
    partial_value = share_partial(
        hidden, my_index, my_keep, base_down, delta_down_in[0], delta_out[0]
    )
    summed = lax.psum_scatter(
        partial_value.reshape(exp_size, base_size, most_rows, model_width).astype(jnp.bfloat16),
        "base",
        scatter_dimension=1,
        tiled=True,
    )
    results = summed.reshape(exp_size, most_rows, model_width)
    returned = lax.all_to_all(results, "exp", split_axis=0, concat_axis=0, tiled=True).reshape(
        exp_size * most_rows, model_width
    )
    gathered = returned[own_targets.reshape(tok_count, choose)]
    combined = jnp.sum(route_weight[:, :, None] * gathered.astype(jnp.float32), axis=1)
    return combined.astype(jnp.bfloat16)


def solution(mesh):
    small = mesh.shape["base"] == 1 and mesh.shape["exp"] == 16
    return jax.shard_map(
        per_device_fused if small else per_device,
        mesh=mesh,
        in_specs=(
            P(("groups", "exp", "base"), None),
            P(("groups", "exp", "base"), None),
            P(("groups", "exp", "base"), None),
            P(),
            P("exp", None, None),
            P("base", None, None, None),
            P("base", None, None, None),
            P("base", None, None, None),
            P("exp", None, None),
            P("exp", None, None, "base"),
            P("exp", "base", None),
            P("exp", None, None),
        ),
        out_specs=P(("groups", "exp", "base"), None),
        check_vma=False,
    )
```

```python
import functools

import jax
import jax.numpy as jnp
from jax import lax
from jax.experimental import pallas as pl
from jax.experimental.pallas import tpu as pltpu
from jax.sharding import PartitionSpec as P

LANES = 128


def fused_kernel(
    nz,
    gather_cuts,
    reduce_cuts,
    tokens_ref,
    weight_ref,
    meta_ref,
    gate_hbm,
    up_hbm,
    down_hbm,
    first_hbm,
    lift_hbm,
    squeeze_hbm,
    last_hbm,
    out_ref,
    tok,
    columns,
    gate_v,
    up_v,
    down_v,
    first_v,
    lift_v,
    squeeze_v,
    last_v,
    hidden,
    segment,
    part,
    scale,
    from_core,
    from_x,
    from_low,
    from_high,
    to_x,
    to_z,
    acc,
    weight_sem,
    gz_recv,
    gx_recv,
    gc_recv,
    gup_send,
    gdown_send,
    gx_send,
    gc_send,
    rc_recv,
    rx_recv,
    rlow_recv,
    rhigh_recv,
    rc_send,
    rx_send,
    rz_send,
):
    rows, width = tokens_ref.shape
    blocks = width // LANES
    pairs = gate_v.shape[0]
    count_blocks = hidden.shape[0]
    per_block = pairs // count_blocks
    all_rows = tok.shape[0]
    me = lax.axis_index("exp")
    core = lax.rem(me, 2)
    x = lax.rem(me // 2, 2)
    z = me // 4

    def place(pz, px, pc):
        return (pz * 2 + px) * 2 + pc

    core_peer = place(z, x, 1 - core)
    x_peer = place(z, 1 - x, core)
    up_peer = me + 4
    down_peer = me - 4
    has_up = z < nz - 1
    has_down = z > 0

    def fetch(position, source, target):
        return pltpu.make_async_copy(source, target, weight_sem.at[position])

    fetches = [
        fetch(0, first_hbm, first_v),
        fetch(1, gate_hbm, gate_v),
        fetch(2, up_hbm, up_v),
        fetch(3, lift_hbm, lift_v),
        fetch(4, down_hbm, down_v),
        fetch(5, squeeze_hbm, squeeze_v),
        fetch(6, last_hbm, last_v),
    ]

    barrier = pltpu.get_barrier_semaphore()

    def greet(peer):
        pl.semaphore_signal(
            barrier, inc=1, device_id={"exp": peer}, device_id_type=pl.DeviceIdType.MESH
        )

    greet(core_peer)
    greet(x_peer)

    @pl.when(has_up)
    def _():
        greet(up_peer)

    @pl.when(has_down)
    def _():
        greet(down_peer)

    own_rows = pl.ds(pl.multiple_of(me * rows, rows), rows)
    tok[own_rows, :width] = tokens_ref[...]
    weights = weight_ref[...]
    lane = lax.broadcasted_iota(jnp.int32, weights.shape, 1)
    high = weights.astype(jnp.bfloat16)
    rest = weights - high.astype(jnp.float32)
    middle = rest.astype(jnp.bfloat16)
    low_part = rest - middle.astype(jnp.float32)
    experts = 4 * nz
    tok[own_rows, width:] = jnp.where(
        lane < experts,
        high.astype(jnp.float32),
        jnp.where(lane < 2 * experts, middle.astype(jnp.float32), low_part),
    ).astype(jnp.bfloat16)

    degree = 2 + has_up.astype(jnp.int32) + has_down.astype(jnp.int32)
    pl.semaphore_wait(barrier, degree)

    def remote(source, target, send, recv, peer):
        return pltpu.make_async_remote_copy(
            src_ref=source,
            dst_ref=target,
            send_sem=send,
            recv_sem=recv,
            device_id={"exp": peer},
            device_id_type=pl.DeviceIdType.MESH,
        )

    all_blocks = blocks + 1
    edges = [(part * all_blocks // gather_cuts) * LANES for part in range(gather_cuts + 1)]
    gather_parts = range(gather_cuts)

    def block_of(pz, px, pc, cut):
        at = pl.ds(pl.multiple_of(place(pz, px, pc) * rows, rows), rows)
        return tok.at[at, pl.ds(edges[cut], edges[cut + 1] - edges[cut])]

    def g_up(pz, cut):
        b = block_of(pz, x, core, cut)
        return remote(b, b, gup_send.at[pz, cut], gz_recv.at[pz, cut], up_peer)

    def g_down(pz, cut):
        b = block_of(pz, x, core, cut)
        return remote(b, b, gdown_send.at[pz, cut], gz_recv.at[pz, cut], down_peer)

    def g_x(pz, px, cut):
        b = block_of(pz, px, core, cut)
        return remote(b, b, gx_send.at[pz, cut], gx_recv.at[pz, cut], x_peer)

    def g_core(pz, px, pc, cut):
        b = block_of(pz, px, pc, cut)
        return remote(b, b, gc_send.at[pz, px, cut], gc_recv.at[pz, px, cut], core_peer)

    def both_sides(distance, act):
        @pl.when(z >= distance)
        def _():
            act(z - distance, True)

        @pl.when(z + distance < nz)
        def _():
            act(z + distance, False)

    def spread_x(pz, cut):
        g_x(pz, x, cut).start()
        g_core(pz, x, core, cut).start()

    def pass_on(cut, pz, upward):
        if upward:
            g_up(pz, cut).wait_recv()

            @pl.when(has_up)
            def _():
                g_up(pz, cut).start()
        else:
            g_down(pz, cut).wait_recv()

            @pl.when(has_down)
            def _():
                g_down(pz, cut).start()
        spread_x(pz, cut)

    def cross(cut, pz, upward=True):
        g_x(pz, 1 - x, cut).wait_recv()
        g_core(pz, 1 - x, core, cut).start()

    def at_distance(distance, act, cut):
        if distance == 0:
            act(cut, z)
        else:
            both_sides(distance, functools.partial(act, cut))

    for cut in gather_parts:

        @pl.when(has_up)
        def _():
            g_up(z, cut).start()

        @pl.when(has_down)
        def _():
            g_down(z, cut).start()

        spread_x(z, cut)
    for one in fetches:
        one.start()
    half_rows = all_rows // 2
    own_half = z // (nz // 2)
    other_half = 1 - own_half

    def half_at(half):
        return pl.ds(pl.multiple_of(half * half_rows, half_rows), half_rows)

    def core_arrived(half):
        for step in range(nz // 2):
            for px in range(2):
                for cut in gather_parts:
                    g_core(half * (nz // 2) + step, px, 1 - core, cut).wait_recv()

    depth = 8 * LANES if blocks % 8 == 0 else LANES

    def keep_tile(value):
        some = jnp.full((16, LANES), value.astype(jnp.float32)).astype(jnp.bfloat16)
        return jnp.concatenate([some] * (LANES // 16), axis=0)

    def compute_hidden(half, meanwhile=None):
        at_rows = half_at(half)
        sent = tok[at_rows, width:].astype(jnp.float32)
        lane = lax.broadcasted_iota(jnp.int32, sent.shape, 1)
        mine = jnp.logical_and(lax.rem(lane, experts) == me, lane < 3 * experts)
        column = jnp.sum(jnp.where(mine, sent, 0.0), axis=1, keepdims=True)
        scale[...] = jnp.broadcast_to(column, scale.shape)

        def column_step(d, carry):
            columns[d] = tok[at_rows, pl.ds(pl.multiple_of(d * LANES, LANES), LANES)]
            return carry

        lax.fori_loop(0, blocks, column_step, 0, unroll=4)

        def low_step(step, total):
            at = pl.ds(pl.multiple_of(step * depth, depth), depth)
            return total + jnp.dot(
                tok[at_rows, at], first_v[at, :], preferred_element_type=jnp.float32
            )

        low = lax.fori_loop(
            0, width // depth, low_step, jnp.zeros((half_rows, LANES), jnp.float32)
        ).astype(jnp.bfloat16)

        if meanwhile is not None:
            meanwhile()

        def hidden_step(f, carry):
            left, right = [], []
            for k in range(per_block):
                pair = f * per_block + k
                left.append(columns[meta_ref[0, pair]])
                keep = keep_tile(meta_ref[1, pair])
                right.append(jnp.concatenate([gate_v[pair] * keep, up_v[pair] * keep], axis=1))
            units = pl.ds(pl.multiple_of(f * LANES, LANES), LANES)
            left.append(low)
            right.append(jnp.concatenate([lift_v[0, :, units], lift_v[1, :, units]], axis=1))
            both = jnp.dot(
                jnp.concatenate(left, axis=1),
                jnp.concatenate(right, axis=0),
                preferred_element_type=jnp.float32,
            )
            gate, up = both[:, :LANES], both[:, LANES:]
            hidden[f] = (gate / (1.0 + jnp.exp(-gate)) * up).astype(jnp.bfloat16)
            return carry

        lax.fori_loop(0, count_blocks, hidden_step, 0, unroll=2)

    def compute_part(half):
        at_rows = half_at(half)

        def squeeze_step(f, total):
            at = pl.ds(pl.multiple_of(f * LANES, LANES), LANES)
            return total + jnp.dot(hidden[f], squeeze_v[at, :], preferred_element_type=jnp.float32)

        squeezed = lax.fori_loop(
            0, count_blocks, squeeze_step, jnp.zeros((half_rows, LANES), jnp.float32), unroll=8
        ).astype(jnp.bfloat16)

        def down_step(step, total):
            pair = meta_ref[2, step]
            tile = down_v[pair] * keep_tile(meta_ref[4, step])
            again = meta_ref[5, step].astype(jnp.float32)
            total = total * again + jnp.dot(
                hidden[meta_ref[3, step]], tile, preferred_element_type=jnp.float32
            )
            segment[step] = total
            return total

        lax.fori_loop(
            0, pairs, down_step, jnp.zeros((half_rows, LANES), jnp.float32), unroll=8
        )

        def output_step(d, carry):
            at = pl.ds(pl.multiple_of(d * LANES, LANES), LANES)
            value = jnp.dot(squeezed, last_v[:, at], preferred_element_type=jnp.float32)
            value = value + segment[meta_ref[6, d]] * meta_ref[7, d].astype(jnp.float32)
            value = value.astype(jnp.bfloat16).astype(jnp.float32) * scale[...]
            part[at_rows, at] = value.astype(jnp.bfloat16)
            return carry

        lax.fori_loop(0, blocks, output_step, 0, unroll=4)

    for distance in range(1, nz - 1):
        for cut in gather_parts:
            at_distance(distance, pass_on, cut)
            at_distance(distance - 1, cross, cut)
    core_arrived(own_half)
    for one in fetches[:4]:
        one.wait()

    compute_hidden(own_half)
    for cut in gather_parts:
        at_distance(nz - 1, pass_on, cut)
        at_distance(nz - 2, cross, cut)
    for one in fetches[4:]:
        one.wait()
    compute_part(own_half)
    for cut in gather_parts:
        at_distance(nz - 1, cross, cut)
    core_arrived(other_half)

    def part_of(pz, px, pc):
        return part.at[pl.ds(pl.multiple_of(place(pz, px, pc) * rows, rows), rows)]

    def r_core(pz, px):
        return remote(
            part_of(pz, px, 1 - core),
            from_core.at[pz, px],
            rc_send.at[pz, px],
            rc_recv.at[pz, px],
            core_peer,
        )

    step_width = width // reduce_cuts
    reduce_parts = range(reduce_cuts)

    def columns_of(cut):
        return pl.ds(cut * step_width, step_width)

    def r_x(pz, cut):
        at = columns_of(cut)
        return remote(
            to_x.at[pz, :, at],
            from_x.at[pz, :, at],
            rx_send.at[pz, cut],
            rx_recv.at[pz, cut],
            x_peer,
        )

    def r_up(pz, cut):
        at = columns_of(cut)
        return remote(
            to_z.at[pz, :, at],
            from_low.at[pz, :, at],
            rz_send.at[pz, cut],
            rlow_recv.at[pz, cut],
            up_peer,
        )

    def r_down(pz, cut):
        at = columns_of(cut)
        return remote(
            to_z.at[pz, :, at],
            from_high.at[pz, :, at],
            rz_send.at[pz, cut],
            rhigh_recv.at[pz, cut],
            down_peer,
        )

    def wide(value):
        return value.astype(jnp.float32)

    def core_start(pz, px):
        r_core(pz, px).start()

    mate = own_half * nz + nz // 2 - 1 - z
    toward = 1 - 2 * own_half
    near = jnp.where(own_half == 0, nz // 2, nz // 2 - 1)
    far = near + toward * (nz // 2 - 1)
    at_end = jnp.logical_or(z == 0, z == nz - 1)

    def part_at(pz, px, cut):
        at = pl.ds(pl.multiple_of(place(pz, px, core) * rows, rows), rows)
        return wide(part[at, columns_of(cut)])

    def x_start(pz):
        r_core(pz, 1 - x).wait_recv()
        for cut in reduce_parts:
            at = columns_of(cut)
            total = part_at(pz, 1 - x, cut) + wide(from_core[pz, 1 - x, :, at])
            to_x[pz, :, at] = total.astype(jnp.bfloat16)
            r_x(pz, cut).start()

    def local_sum(pz, cut):
        r_x(pz, cut).wait_recv()
        at = columns_of(cut)
        total = part_at(pz, x, cut) + wide(from_core[pz, x, :, at])
        return total + wide(from_x[pz, :, at])

    def z_step(pz):
        r_core(pz, x).wait_recv()
        for cut in reduce_parts:
            at = columns_of(cut)
            acc[:, at] = local_sum(pz, cut)

            @pl.when(pz < z)
            def _():
                @pl.when(has_up)
                def _():
                    r_down(pz, cut).wait_recv()
                    acc[:, at] += wide(from_high[pz, :, at])

                to_z[pz, :, at] = acc[:, at].astype(jnp.bfloat16)
                r_down(pz, cut).start()

            @pl.when(pz > z)
            def _():
                @pl.when(has_down)
                def _():
                    r_up(pz, cut).wait_recv()
                    acc[:, at] += wide(from_low[pz, :, at])

                to_z[pz, :, at] = acc[:, at].astype(jnp.bfloat16)
                r_up(pz, cut).start()

    for px in (1 - x, x):
        core_start(mate, px)
        core_start(z, px)

    def near_sums():
        x_start(mate)
        x_start(z)

    compute_hidden(other_half, near_sums)
    compute_part(other_half)
    for px in (1 - x, x):
        core_start(far, px)
        core_start(near, px)

    x_start(far)
    x_start(near)

    @pl.when(at_end)
    def _():
        z_step(mate)

    z_step(far)

    @pl.when(jnp.logical_not(at_end))
    def _():
        z_step(mate)

    z_step(near)
    r_core(z, x).wait_recv()
    for cut in reduce_parts:
        at = columns_of(cut)
        acc[:, at] = local_sum(z, cut)

        @pl.when(has_up)
        def _():
            r_down(z, cut).wait_recv()
            acc[:, at] += wide(from_high[z, :, at])

        @pl.when(has_down)
        def _():
            r_up(z, cut).wait_recv()
            acc[:, at] += wide(from_low[z, :, at])

        out_ref[:, at] = acc[:, at].astype(jnp.bfloat16)

    for pz in range(nz):
        for px in range(2):
            r_core(pz, px).wait_send()
        for cut in reduce_parts:
            r_x(pz, cut).wait_send()

            @pl.when(pz != z)
            def _():
                r_up(pz, cut).wait_send()

    for pz in range(nz):
        for cut in gather_parts:

            @pl.when(jnp.logical_and(has_up, pz <= z))
            def _():
                g_up(pz, cut).wait_send()

            @pl.when(jnp.logical_and(has_down, pz >= z))
            def _():
                g_down(pz, cut).wait_send()

            g_x(pz, x, cut).wait_send()
            for px in range(2):
                g_core(pz, px, core, cut).wait_send()


def tile_plan(base_index, keep, blocks):
    flat = base_index.reshape(-1)
    pairs = flat.shape[0]
    place = jnp.arange(pairs, dtype=jnp.int32)
    ahead = (flat[:, None] < flat[None, :]) | (
        (flat[:, None] == flat[None, :]) & (place[:, None] < place[None, :])
    )
    rank = jnp.sum(ahead.astype(jnp.int32), axis=0)
    chosen = (rank[:, None] == place[None, :]).astype(jnp.int32)
    keep = keep.reshape(-1)
    order = jnp.sum(chosen * place[:, None], axis=0)
    sorted_keep = jnp.sum(chosen * keep[:, None], axis=0)
    sorted_block = jnp.sum(chosen * flat[:, None], axis=0)
    again = jnp.concatenate(
        [jnp.zeros((1,), jnp.int32), (sorted_block[1:] == sorted_block[:-1]).astype(jnp.int32)]
    )
    block = jnp.arange(blocks, dtype=jnp.int32)
    upto = jnp.sum((flat[:, None] <= block[None, :]).astype(jnp.int32), axis=0)
    used = jnp.any(flat[:, None] == block[None, :], axis=0).astype(jnp.int32)
    size = max(pairs, blocks)

    def row(values):
        return jnp.pad(values, (0, size - values.shape[0]))

    return jnp.stack(
        [
            row(flat),
            row(keep),
            row(order),
            row(order // base_index.shape[1]),
            row(sorted_keep),
            row(again),
            row(jnp.maximum(upto - 1, 0)),
            row(used),
        ]
    )


def per_device_fused(
    tokens,
    routes,
    route_weight,
    base_index,
    expert_mask,
    base_gate,
    base_up,
    base_down,
    delta_in,
    delta_gate_up,
    delta_down_in,
    delta_out,
):
    rows, width = tokens.shape
    experts = lax.axis_size("exp")
    nz = experts // 4
    blocks = width // LANES
    count_blocks, per_block = base_index.shape
    pairs = count_blocks * per_block
    all_rows = rows * experts
    named = routes[:, :, None] == jnp.arange(experts, dtype=jnp.int32)[None, None, :]
    weights = jnp.sum(jnp.where(named, route_weight[:, :, None], 0.0), axis=1)
    weights = jnp.pad(
        jnp.concatenate([weights] * 3, axis=1), ((0, 0), (0, LANES - 3 * experts))
    )
    meta = tile_plan(base_index, expert_mask[0], blocks)
    lift = delta_gate_up[0]
    units = lift.shape[2]
    bf16, f32 = jnp.bfloat16, jnp.float32
    vmem, smem, anywhere = (
        pl.BlockSpec(memory_space=space) for space in (pltpu.VMEM, pltpu.SMEM, pl.ANY)
    )
    dma = pltpu.SemaphoreType.DMA
    gather_cuts = 2
    reduce_cuts = 4 if blocks % 4 == 0 else 1
    return pl.pallas_call(
        functools.partial(fused_kernel, nz, gather_cuts, reduce_cuts),
        out_shape=jax.ShapeDtypeStruct((rows, width), bf16),
        in_specs=[vmem, vmem, smem] + [anywhere] * 7,
        out_specs=vmem,
        scratch_shapes=[
            pltpu.VMEM((all_rows, width + LANES), bf16),
            pltpu.VMEM((blocks, all_rows // 2, LANES), bf16),
            pltpu.VMEM((pairs, LANES, LANES), bf16),
            pltpu.VMEM((pairs, LANES, LANES), bf16),
            pltpu.VMEM((pairs, LANES, LANES), bf16),
            pltpu.VMEM((width, LANES), bf16),
            pltpu.VMEM((2, LANES, units), bf16),
            pltpu.VMEM((units, LANES), bf16),
            pltpu.VMEM((LANES, width), bf16),
            pltpu.VMEM((count_blocks, all_rows // 2, LANES), bf16),
            pltpu.VMEM((pairs, all_rows // 2, LANES), f32),
            pltpu.VMEM((all_rows, width), bf16),
            pltpu.VMEM((all_rows // 2, LANES), f32),
            pltpu.VMEM((nz, 2, rows, width), bf16),
            pltpu.VMEM((nz, rows, width), bf16),
            pltpu.VMEM((nz, rows, width), bf16),
            pltpu.VMEM((nz, rows, width), bf16),
            pltpu.VMEM((nz, rows, width), bf16),
            pltpu.VMEM((nz, rows, width), bf16),
            pltpu.VMEM((rows, width), f32),
            dma((7,)),
            dma((nz, gather_cuts)),
            dma((nz, gather_cuts)),
            dma((nz, 2, gather_cuts)),
            dma((nz, gather_cuts)),
            dma((nz, gather_cuts)),
            dma((nz, gather_cuts)),
            dma((nz, 2, gather_cuts)),
            dma((nz, 2)),
            dma((nz, reduce_cuts)),
            dma((nz, reduce_cuts)),
            dma((nz, reduce_cuts)),
            dma((nz, 2)),
            dma((nz, reduce_cuts)),
            dma((nz, reduce_cuts)),
        ],
        compiler_params=pltpu.CompilerParams(
            collective_id=0, has_side_effects=True, vmem_limit_bytes=60 << 20
        ),
        name="expert_layer",
    )(
        tokens,
        weights,
        meta,
        base_gate.reshape(pairs, LANES, LANES),
        base_up.reshape(pairs, LANES, LANES),
        base_down.reshape(pairs, LANES, LANES),
        delta_in[0],
        lift,
        delta_down_in[0],
        delta_out[0],
    )


def place_rows(route_block, experts, most_rows, copies, copy_index):
    flat_routes = route_block.reshape(-1)
    onehot = (flat_routes[:, None] == jnp.arange(experts, dtype=jnp.int32)[None, :]).astype(
        jnp.int32
    )
    before = jnp.cumsum(onehot, axis=0) - onehot
    slot_index = jnp.sum(before * onehot, axis=1)
    return (flat_routes * copies + copy_index) * most_rows + slot_index


def spread_matrix(targets, slot_count, choose):
    matches = targets[None, :] == jnp.arange(slot_count, dtype=jnp.int32)[:, None]
    return jnp.any(matches.reshape(slot_count, -1, choose), axis=2).astype(jnp.bfloat16)


def hidden_units(incoming, index_part, keep_part, gate_tiles, up_tiles, delta_first, lift):
    row_count, model_width = incoming.shape
    blocks = model_width // 128
    count_blocks, per_block = index_part.shape
    picked = jnp.take(incoming.reshape(row_count, blocks, 128), index_part.reshape(-1), axis=1)
    picked = picked.reshape(row_count, count_blocks, per_block, 128)
    tile_keep = keep_part.astype(jnp.bfloat16)[:, :, None, None]
    pre_gate = jnp.einsum(
        "rfkc,fkch->rfh", picked, gate_tiles * tile_keep, preferred_element_type=jnp.float32
    ).reshape(row_count, -1)
    pre_up = jnp.einsum(
        "rfkc,fkch->rfh", picked, up_tiles * tile_keep, preferred_element_type=jnp.float32
    ).reshape(row_count, -1)
    lowrank = jnp.dot(incoming, delta_first, preferred_element_type=jnp.float32).astype(
        jnp.bfloat16
    )
    lifted = jnp.einsum("rq,gqh->grh", lowrank, lift, preferred_element_type=jnp.float32)
    return (jax.nn.silu(pre_gate + lifted[0]) * (pre_up + lifted[1])).astype(jnp.bfloat16)


def share_partial(hidden_part, index_part, keep_part, down_tiles, squeeze, delta_last):
    row_count = hidden_part.shape[0]
    count_blocks = down_tiles.shape[0]
    model_width = delta_last.shape[1]
    tile_keep = keep_part.astype(jnp.bfloat16)[:, :, None, None]
    pieces = jnp.einsum(
        "rfh,fkhc->rfkc",
        hidden_part.reshape(row_count, count_blocks, 128),
        down_tiles * tile_keep,
        preferred_element_type=jnp.float32,
    )
    placed = (
        jnp.zeros((row_count, model_width // 128, 128), jnp.float32)
        .at[:, index_part.reshape(-1)]
        .add(pieces.reshape(row_count, -1, 128))
    )
    squeezed = jnp.dot(hidden_part, squeeze, preferred_element_type=jnp.float32).astype(
        jnp.bfloat16
    )
    return placed.reshape(row_count, model_width) + jnp.dot(
        squeezed, delta_last, preferred_element_type=jnp.float32
    )


def per_device(
    tokens,
    routes,
    route_weight,
    base_index,
    expert_mask,
    base_gate,
    base_up,
    base_down,
    delta_in,
    delta_gate_up,
    delta_down_in,
    delta_out,
):
    tok_count, model_width = tokens.shape
    choose = routes.shape[1]
    exp_size = lax.axis_size("exp")
    base_size = lax.axis_size("base")
    half_blocks = base_gate.shape[0]
    most_rows = min(tok_count, max(2, (tok_count * choose + exp_size - 1) // exp_size * 3 // 2))
    own_targets = place_rows(routes, exp_size, most_rows, 1, 0)
    offset = lax.axis_index("base") * half_blocks
    my_index = lax.dynamic_slice_in_dim(base_index, offset, half_blocks, 0)
    my_keep = lax.dynamic_slice_in_dim(expert_mask[0], offset, half_blocks, 0)
    pair_tokens, pair_routes = (
        lax.all_gather(tokens, "base", axis=0, tiled=True),
        lax.all_gather(routes.astype(jnp.bfloat16), "base", axis=0, tiled=True),
    )
    pair_routes = pair_routes.astype(jnp.int32)
    targets = jnp.concatenate(
        [
            place_rows(
                pair_routes[copy_index * tok_count : (copy_index + 1) * tok_count],
                exp_size,
                most_rows,
                base_size,
                copy_index,
            )
            for copy_index in range(base_size)
        ]
    )
    spread = spread_matrix(targets, exp_size * base_size * most_rows, choose)
    outgoing = jnp.dot(spread, pair_tokens, preferred_element_type=jnp.float32).astype(jnp.bfloat16)
    outgoing = outgoing.reshape(exp_size, base_size * most_rows, model_width)
    arrived = lax.all_to_all(outgoing, "exp", split_axis=0, concat_axis=0, tiled=True)
    incoming = arrived.reshape(-1, model_width)
    hidden = hidden_units(
        incoming, my_index, my_keep, base_gate, base_up, delta_in[0], delta_gate_up[0]
    )
    partial_value = share_partial(
        hidden, my_index, my_keep, base_down, delta_down_in[0], delta_out[0]
    )
    summed = lax.psum_scatter(
        partial_value.reshape(exp_size, base_size, most_rows, model_width).astype(jnp.bfloat16),
        "base",
        scatter_dimension=1,
        tiled=True,
    )
    results = summed.reshape(exp_size, most_rows, model_width)
    returned = lax.all_to_all(results, "exp", split_axis=0, concat_axis=0, tiled=True).reshape(
        exp_size * most_rows, model_width
    )
    gathered = returned[own_targets.reshape(tok_count, choose)]
    combined = jnp.sum(route_weight[:, :, None] * gathered.astype(jnp.float32), axis=1)
    return combined.astype(jnp.bfloat16)


def solution(mesh):
    small = mesh.shape["base"] == 1 and mesh.shape["exp"] == 16
    return jax.shard_map(
        per_device_fused if small else per_device,
        mesh=mesh,
        in_specs=(
            P(("groups", "exp", "base"), None),
            P(("groups", "exp", "base"), None),
            P(("groups", "exp", "base"), None),
            P(),
            P("exp", None, None),
            P("base", None, None, None),
            P("base", None, None, None),
            P("base", None, None, None),
            P("exp", None, None),
            P("exp", None, None, "base"),
            P("exp", "base", None),
            P("exp", None, None),
        ),
        out_specs=P(("groups", "exp", "base"), None),
        check_vma=False,
    )
```

```python
import functools

import jax
import jax.numpy as jnp
from jax import lax
from jax.experimental import pallas as pl
from jax.experimental.pallas import tpu as pltpu
from jax.sharding import PartitionSpec as P

LANES = 128


def fused_kernel(
    nz,
    gather_cuts,
    reduce_cuts,
    tokens_ref,
    weight_ref,
    meta_ref,
    gate_hbm,
    up_hbm,
    down_hbm,
    first_hbm,
    lift_hbm,
    squeeze_hbm,
    last_hbm,
    out_ref,
    tok,
    columns,
    gate_v,
    up_v,
    down_v,
    first_v,
    lift_v,
    squeeze_v,
    last_v,
    hidden,
    segment,
    part,
    scale,
    from_core,
    from_x,
    from_low,
    from_high,
    to_x,
    to_z,
    acc,
    weight_sem,
    gz_recv,
    gx_recv,
    gc_recv,
    gup_send,
    gdown_send,
    gx_send,
    gc_send,
    rc_recv,
    rx_recv,
    rlow_recv,
    rhigh_recv,
    rc_send,
    rx_send,
    rz_send,
):
    rows, width = tokens_ref.shape
    blocks = width // LANES
    pairs = gate_v.shape[0]
    count_blocks = hidden.shape[0]
    per_block = pairs // count_blocks
    all_rows = tok.shape[0]
    me = lax.axis_index("exp")
    core = lax.rem(me, 2)
    x = lax.rem(me // 2, 2)
    z = me // 4

    def place(pz, px, pc):
        return (pz * 2 + px) * 2 + pc

    core_peer = place(z, x, 1 - core)
    x_peer = place(z, 1 - x, core)
    up_peer = me + 4
    down_peer = me - 4
    has_up = z < nz - 1
    has_down = z > 0

    def fetch(position, source, target):
        return pltpu.make_async_copy(source, target, weight_sem.at[position])

    fetches = [
        fetch(0, first_hbm, first_v),
        fetch(1, gate_hbm, gate_v),
        fetch(2, up_hbm, up_v),
        fetch(3, lift_hbm, lift_v),
        fetch(4, down_hbm, down_v),
        fetch(5, squeeze_hbm, squeeze_v),
        fetch(6, last_hbm, last_v),
    ]

    barrier = pltpu.get_barrier_semaphore()

    def greet(peer):
        pl.semaphore_signal(
            barrier, inc=1, device_id={"exp": peer}, device_id_type=pl.DeviceIdType.MESH
        )

    greet(core_peer)
    greet(x_peer)

    @pl.when(has_up)
    def _():
        greet(up_peer)

    @pl.when(has_down)
    def _():
        greet(down_peer)

    own_rows = pl.ds(pl.multiple_of(me * rows, rows), rows)
    tok[own_rows, :width] = tokens_ref[...]
    weights = weight_ref[...]
    lane = lax.broadcasted_iota(jnp.int32, weights.shape, 1)
    high = weights.astype(jnp.bfloat16)
    rest = weights - high.astype(jnp.float32)
    middle = rest.astype(jnp.bfloat16)
    low_part = rest - middle.astype(jnp.float32)
    experts = 4 * nz
    tok[own_rows, width:] = jnp.where(
        lane < experts,
        high.astype(jnp.float32),
        jnp.where(lane < 2 * experts, middle.astype(jnp.float32), low_part),
    ).astype(jnp.bfloat16)

    degree = 2 + has_up.astype(jnp.int32) + has_down.astype(jnp.int32)
    pl.semaphore_wait(barrier, degree)

    def remote(source, target, send, recv, peer):
        return pltpu.make_async_remote_copy(
            src_ref=source,
            dst_ref=target,
            send_sem=send,
            recv_sem=recv,
            device_id={"exp": peer},
            device_id_type=pl.DeviceIdType.MESH,
        )

    all_blocks = blocks + 1
    edges = [(part * all_blocks // gather_cuts) * LANES for part in range(gather_cuts + 1)]
    gather_parts = range(gather_cuts)

    def block_of(pz, px, pc, cut):
        at = pl.ds(pl.multiple_of(place(pz, px, pc) * rows, rows), rows)
        return tok.at[at, pl.ds(edges[cut], edges[cut + 1] - edges[cut])]

    def g_up(pz, cut):
        b = block_of(pz, x, core, cut)
        return remote(b, b, gup_send.at[pz, cut], gz_recv.at[pz, cut], up_peer)

    def g_down(pz, cut):
        b = block_of(pz, x, core, cut)
        return remote(b, b, gdown_send.at[pz, cut], gz_recv.at[pz, cut], down_peer)

    def g_x(pz, px, cut):
        b = block_of(pz, px, core, cut)
        return remote(b, b, gx_send.at[pz, cut], gx_recv.at[pz, cut], x_peer)

    def g_core(pz, px, pc, cut):
        b = block_of(pz, px, pc, cut)
        return remote(b, b, gc_send.at[pz, px, cut], gc_recv.at[pz, px, cut], core_peer)

    def both_sides(distance, act):
        @pl.when(z >= distance)
        def _():
            act(z - distance, True)

        @pl.when(z + distance < nz)
        def _():
            act(z + distance, False)

    def spread_x(pz, cut):
        g_x(pz, x, cut).start()
        g_core(pz, x, core, cut).start()

    def pass_on(cut, pz, upward):
        if upward:
            g_up(pz, cut).wait_recv()

            @pl.when(has_up)
            def _():
                g_up(pz, cut).start()
        else:
            g_down(pz, cut).wait_recv()

            @pl.when(has_down)
            def _():
                g_down(pz, cut).start()
        spread_x(pz, cut)

    def cross(cut, pz, upward=True):
        g_x(pz, 1 - x, cut).wait_recv()
        g_core(pz, 1 - x, core, cut).start()

    def at_distance(distance, act, cut):
        if distance == 0:
            act(cut, z)
        else:
            both_sides(distance, functools.partial(act, cut))

    for cut in gather_parts:

        @pl.when(has_up)
        def _():
            g_up(z, cut).start()

        @pl.when(has_down)
        def _():
            g_down(z, cut).start()

        spread_x(z, cut)
    for one in fetches:
        one.start()
    half_rows = all_rows // 2
    own_half = z // (nz // 2)
    other_half = 1 - own_half

    def half_at(half):
        return pl.ds(pl.multiple_of(half * half_rows, half_rows), half_rows)

    def core_arrived(half):
        for step in range(nz // 2):
            for px in range(2):
                for cut in gather_parts:
                    g_core(half * (nz // 2) + step, px, 1 - core, cut).wait_recv()

    depth = 8 * LANES if blocks % 8 == 0 else LANES

    def keep_tile(value):
        some = jnp.full((16, LANES), value.astype(jnp.float32)).astype(jnp.bfloat16)
        return jnp.concatenate([some] * (LANES // 16), axis=0)

    def compute_hidden(half):
        at_rows = half_at(half)
        sent = tok[at_rows, width:].astype(jnp.float32)
        lane = lax.broadcasted_iota(jnp.int32, sent.shape, 1)
        mine = jnp.logical_and(lax.rem(lane, experts) == me, lane < 3 * experts)
        column = jnp.sum(jnp.where(mine, sent, 0.0), axis=1, keepdims=True)
        scale[...] = jnp.broadcast_to(column, scale.shape)

        def column_step(d, carry):
            columns[d] = tok[at_rows, pl.ds(pl.multiple_of(d * LANES, LANES), LANES)]
            return carry

        lax.fori_loop(0, blocks, column_step, 0, unroll=4)

        def low_step(step, total):
            at = pl.ds(pl.multiple_of(step * depth, depth), depth)
            return total + jnp.dot(
                tok[at_rows, at], first_v[at, :], preferred_element_type=jnp.float32
            )

        low = lax.fori_loop(
            0, width // depth, low_step, jnp.zeros((half_rows, LANES), jnp.float32)
        ).astype(jnp.bfloat16)

        def hidden_step(f, carry):
            left, right = [], []
            for k in range(per_block):
                pair = f * per_block + k
                left.append(columns[meta_ref[0, pair]])
                keep = keep_tile(meta_ref[1, pair])
                right.append(jnp.concatenate([gate_v[pair] * keep, up_v[pair] * keep], axis=1))
            units = pl.ds(pl.multiple_of(f * LANES, LANES), LANES)
            left.append(low)
            right.append(jnp.concatenate([lift_v[0, :, units], lift_v[1, :, units]], axis=1))
            both = jnp.dot(
                jnp.concatenate(left, axis=1),
                jnp.concatenate(right, axis=0),
                preferred_element_type=jnp.float32,
            )
            gate, up = both[:, :LANES], both[:, LANES:]
            hidden[f] = (gate / (1.0 + jnp.exp(-gate)) * up).astype(jnp.bfloat16)
            return carry

        lax.fori_loop(0, count_blocks, hidden_step, 0, unroll=2)

    def compute_part(half):
        at_rows = half_at(half)

        def squeeze_step(f, total):
            at = pl.ds(pl.multiple_of(f * LANES, LANES), LANES)
            return total + jnp.dot(hidden[f], squeeze_v[at, :], preferred_element_type=jnp.float32)

        squeezed = lax.fori_loop(
            0, count_blocks, squeeze_step, jnp.zeros((half_rows, LANES), jnp.float32), unroll=8
        ).astype(jnp.bfloat16)

        def down_step(step, total):
            pair = meta_ref[2, step]
            tile = down_v[pair] * keep_tile(meta_ref[4, step])
            again = meta_ref[5, step].astype(jnp.float32)
            total = total * again + jnp.dot(
                hidden[meta_ref[3, step]], tile, preferred_element_type=jnp.float32
            )
            segment[step] = total
            return total

        lax.fori_loop(
            0, pairs, down_step, jnp.zeros((half_rows, LANES), jnp.float32), unroll=8
        )

        def output_step(d, carry):
            at = pl.ds(pl.multiple_of(d * LANES, LANES), LANES)
            value = jnp.dot(squeezed, last_v[:, at], preferred_element_type=jnp.float32)
            value = value + segment[meta_ref[6, d]] * meta_ref[7, d].astype(jnp.float32)
            value = value.astype(jnp.bfloat16).astype(jnp.float32) * scale[...]
            part[at_rows, at] = value.astype(jnp.bfloat16)
            return carry

        lax.fori_loop(0, blocks, output_step, 0, unroll=4)

    for distance in range(1, nz - 1):
        for cut in gather_parts:
            at_distance(distance, pass_on, cut)
            at_distance(distance - 1, cross, cut)
    core_arrived(own_half)
    for one in fetches[:4]:
        one.wait()

    compute_hidden(own_half)
    for cut in gather_parts:
        at_distance(nz - 1, pass_on, cut)
        at_distance(nz - 2, cross, cut)
    for one in fetches[4:]:
        one.wait()
    compute_part(own_half)

    def part_of(pz, px, pc):
        return part.at[pl.ds(pl.multiple_of(place(pz, px, pc) * rows, rows), rows)]

    def r_core(pz, px):
        return remote(
            part_of(pz, px, 1 - core),
            from_core.at[pz, px],
            rc_send.at[pz, px],
            rc_recv.at[pz, px],
            core_peer,
        )

    step_width = width // reduce_cuts
    reduce_parts = range(reduce_cuts)

    def columns_of(cut):
        return pl.ds(cut * step_width, step_width)

    def r_x(pz, cut):
        at = columns_of(cut)
        return remote(
            to_x.at[pz, :, at],
            from_x.at[pz, :, at],
            rx_send.at[pz, cut],
            rx_recv.at[pz, cut],
            x_peer,
        )

    def r_up(pz, cut):
        at = columns_of(cut)
        return remote(
            to_z.at[pz, :, at],
            from_low.at[pz, :, at],
            rz_send.at[pz, cut],
            rlow_recv.at[pz, cut],
            up_peer,
        )

    def r_down(pz, cut):
        at = columns_of(cut)
        return remote(
            to_z.at[pz, :, at],
            from_high.at[pz, :, at],
            rz_send.at[pz, cut],
            rhigh_recv.at[pz, cut],
            down_peer,
        )

    def wide(value):
        return value.astype(jnp.float32)

    def core_start(pz, px):
        r_core(pz, px).start()

    mate = own_half * nz + nz // 2 - 1 - z
    toward = 1 - 2 * own_half
    near = jnp.where(own_half == 0, nz // 2, nz // 2 - 1)
    far = near + toward * (nz // 2 - 1)
    at_end = jnp.logical_or(z == 0, z == nz - 1)

    def part_at(pz, px, cut):
        at = pl.ds(pl.multiple_of(place(pz, px, core) * rows, rows), rows)
        return wide(part[at, columns_of(cut)])

    def x_start(pz):
        r_core(pz, 1 - x).wait_recv()
        for cut in reduce_parts:
            at = columns_of(cut)
            total = part_at(pz, 1 - x, cut) + wide(from_core[pz, 1 - x, :, at])
            to_x[pz, :, at] = total.astype(jnp.bfloat16)
            r_x(pz, cut).start()

    def local_sum(pz, cut):
        r_x(pz, cut).wait_recv()
        at = columns_of(cut)
        total = part_at(pz, x, cut) + wide(from_core[pz, x, :, at])
        return total + wide(from_x[pz, :, at])

    def z_step(pz):
        r_core(pz, x).wait_recv()
        for cut in reduce_parts:
            at = columns_of(cut)
            acc[:, at] = local_sum(pz, cut)

            @pl.when(pz < z)
            def _():
                @pl.when(has_up)
                def _():
                    r_down(pz, cut).wait_recv()
                    acc[:, at] += wide(from_high[pz, :, at])

                to_z[pz, :, at] = acc[:, at].astype(jnp.bfloat16)
                r_down(pz, cut).start()

            @pl.when(pz > z)
            def _():
                @pl.when(has_down)
                def _():
                    r_up(pz, cut).wait_recv()
                    acc[:, at] += wide(from_low[pz, :, at])

                to_z[pz, :, at] = acc[:, at].astype(jnp.bfloat16)
                r_up(pz, cut).start()

    for px in (1 - x, x):
        core_start(mate, px)
        core_start(z, px)
    for cut in gather_parts:
        at_distance(nz - 1, cross, cut)
    x_start(mate)
    x_start(z)
    core_arrived(other_half)
    compute_hidden(other_half)
    compute_part(other_half)
    for px in (1 - x, x):
        core_start(far, px)
        core_start(near, px)

    x_start(far)
    x_start(near)

    @pl.when(at_end)
    def _():
        z_step(mate)

    z_step(far)

    @pl.when(jnp.logical_not(at_end))
    def _():
        z_step(mate)

    z_step(near)
    r_core(z, x).wait_recv()
    for cut in reduce_parts:
        at = columns_of(cut)
        acc[:, at] = local_sum(z, cut)

        @pl.when(has_up)
        def _():
            r_down(z, cut).wait_recv()
            acc[:, at] += wide(from_high[z, :, at])

        @pl.when(has_down)
        def _():
            r_up(z, cut).wait_recv()
            acc[:, at] += wide(from_low[z, :, at])

        out_ref[:, at] = acc[:, at].astype(jnp.bfloat16)

    for pz in range(nz):
        for px in range(2):
            r_core(pz, px).wait_send()
        for cut in reduce_parts:
            r_x(pz, cut).wait_send()

            @pl.when(pz != z)
            def _():
                r_up(pz, cut).wait_send()

    for pz in range(nz):
        for cut in gather_parts:

            @pl.when(jnp.logical_and(has_up, pz <= z))
            def _():
                g_up(pz, cut).wait_send()

            @pl.when(jnp.logical_and(has_down, pz >= z))
            def _():
                g_down(pz, cut).wait_send()

            g_x(pz, x, cut).wait_send()
            for px in range(2):
                g_core(pz, px, core, cut).wait_send()


def tile_plan(base_index, keep, blocks):
    flat = base_index.reshape(-1)
    pairs = flat.shape[0]
    place = jnp.arange(pairs, dtype=jnp.int32)
    ahead = (flat[:, None] < flat[None, :]) | (
        (flat[:, None] == flat[None, :]) & (place[:, None] < place[None, :])
    )
    rank = jnp.sum(ahead.astype(jnp.int32), axis=0)
    chosen = (rank[:, None] == place[None, :]).astype(jnp.int32)
    keep = keep.reshape(-1)
    order = jnp.sum(chosen * place[:, None], axis=0)
    sorted_keep = jnp.sum(chosen * keep[:, None], axis=0)
    sorted_block = jnp.sum(chosen * flat[:, None], axis=0)
    again = jnp.concatenate(
        [jnp.zeros((1,), jnp.int32), (sorted_block[1:] == sorted_block[:-1]).astype(jnp.int32)]
    )
    block = jnp.arange(blocks, dtype=jnp.int32)
    upto = jnp.sum((flat[:, None] <= block[None, :]).astype(jnp.int32), axis=0)
    used = jnp.any(flat[:, None] == block[None, :], axis=0).astype(jnp.int32)
    size = max(pairs, blocks)

    def row(values):
        return jnp.pad(values, (0, size - values.shape[0]))

    return jnp.stack(
        [
            row(flat),
            row(keep),
            row(order),
            row(order // base_index.shape[1]),
            row(sorted_keep),
            row(again),
            row(jnp.maximum(upto - 1, 0)),
            row(used),
        ]
    )


def per_device_fused(
    tokens,
    routes,
    route_weight,
    base_index,
    expert_mask,
    base_gate,
    base_up,
    base_down,
    delta_in,
    delta_gate_up,
    delta_down_in,
    delta_out,
):
    rows, width = tokens.shape
    experts = lax.axis_size("exp")
    nz = experts // 4
    blocks = width // LANES
    count_blocks, per_block = base_index.shape
    pairs = count_blocks * per_block
    all_rows = rows * experts
    named = routes[:, :, None] == jnp.arange(experts, dtype=jnp.int32)[None, None, :]
    weights = jnp.sum(jnp.where(named, route_weight[:, :, None], 0.0), axis=1)
    weights = jnp.pad(
        jnp.concatenate([weights] * 3, axis=1), ((0, 0), (0, LANES - 3 * experts))
    )
    meta = tile_plan(base_index, expert_mask[0], blocks)
    lift = delta_gate_up[0]
    units = lift.shape[2]
    bf16, f32 = jnp.bfloat16, jnp.float32
    vmem, smem, anywhere = (
        pl.BlockSpec(memory_space=space) for space in (pltpu.VMEM, pltpu.SMEM, pl.ANY)
    )
    dma = pltpu.SemaphoreType.DMA
    gather_cuts = 2
    reduce_cuts = 4 if blocks % 4 == 0 else 1
    return pl.pallas_call(
        functools.partial(fused_kernel, nz, gather_cuts, reduce_cuts),
        out_shape=jax.ShapeDtypeStruct((rows, width), bf16),
        in_specs=[vmem, vmem, smem] + [anywhere] * 7,
        out_specs=vmem,
        scratch_shapes=[
            pltpu.VMEM((all_rows, width + LANES), bf16),
            pltpu.VMEM((blocks, all_rows // 2, LANES), bf16),
            pltpu.VMEM((pairs, LANES, LANES), bf16),
            pltpu.VMEM((pairs, LANES, LANES), bf16),
            pltpu.VMEM((pairs, LANES, LANES), bf16),
            pltpu.VMEM((width, LANES), bf16),
            pltpu.VMEM((2, LANES, units), bf16),
            pltpu.VMEM((units, LANES), bf16),
            pltpu.VMEM((LANES, width), bf16),
            pltpu.VMEM((count_blocks, all_rows // 2, LANES), bf16),
            pltpu.VMEM((pairs, all_rows // 2, LANES), f32),
            pltpu.VMEM((all_rows, width), bf16),
            pltpu.VMEM((all_rows // 2, LANES), f32),
            pltpu.VMEM((nz, 2, rows, width), bf16),
            pltpu.VMEM((nz, rows, width), bf16),
            pltpu.VMEM((nz, rows, width), bf16),
            pltpu.VMEM((nz, rows, width), bf16),
            pltpu.VMEM((nz, rows, width), bf16),
            pltpu.VMEM((nz, rows, width), bf16),
            pltpu.VMEM((rows, width), f32),
            dma((7,)),
            dma((nz, gather_cuts)),
            dma((nz, gather_cuts)),
            dma((nz, 2, gather_cuts)),
            dma((nz, gather_cuts)),
            dma((nz, gather_cuts)),
            dma((nz, gather_cuts)),
            dma((nz, 2, gather_cuts)),
            dma((nz, 2)),
            dma((nz, reduce_cuts)),
            dma((nz, reduce_cuts)),
            dma((nz, reduce_cuts)),
            dma((nz, 2)),
            dma((nz, reduce_cuts)),
            dma((nz, reduce_cuts)),
        ],
        compiler_params=pltpu.CompilerParams(
            collective_id=0, has_side_effects=True, vmem_limit_bytes=60 << 20
        ),
        name="expert_layer",
    )(
        tokens,
        weights,
        meta,
        base_gate.reshape(pairs, LANES, LANES),
        base_up.reshape(pairs, LANES, LANES),
        base_down.reshape(pairs, LANES, LANES),
        delta_in[0],
        lift,
        delta_down_in[0],
        delta_out[0],
    )


def place_rows(route_block, experts, most_rows, copies, copy_index):
    flat_routes = route_block.reshape(-1)
    onehot = (flat_routes[:, None] == jnp.arange(experts, dtype=jnp.int32)[None, :]).astype(
        jnp.int32
    )
    before = jnp.cumsum(onehot, axis=0) - onehot
    slot_index = jnp.sum(before * onehot, axis=1)
    return (flat_routes * copies + copy_index) * most_rows + slot_index


def spread_matrix(targets, slot_count, choose):
    matches = targets[None, :] == jnp.arange(slot_count, dtype=jnp.int32)[:, None]
    return jnp.any(matches.reshape(slot_count, -1, choose), axis=2).astype(jnp.bfloat16)


def hidden_units(incoming, index_part, keep_part, gate_tiles, up_tiles, delta_first, lift):
    row_count, model_width = incoming.shape
    blocks = model_width // 128
    count_blocks, per_block = index_part.shape
    picked = jnp.take(incoming.reshape(row_count, blocks, 128), index_part.reshape(-1), axis=1)
    picked = picked.reshape(row_count, count_blocks, per_block, 128)
    tile_keep = keep_part.astype(jnp.bfloat16)[:, :, None, None]
    pre_gate = jnp.einsum(
        "rfkc,fkch->rfh", picked, gate_tiles * tile_keep, preferred_element_type=jnp.float32
    ).reshape(row_count, -1)
    pre_up = jnp.einsum(
        "rfkc,fkch->rfh", picked, up_tiles * tile_keep, preferred_element_type=jnp.float32
    ).reshape(row_count, -1)
    lowrank = jnp.dot(incoming, delta_first, preferred_element_type=jnp.float32).astype(
        jnp.bfloat16
    )
    lifted = jnp.einsum("rq,gqh->grh", lowrank, lift, preferred_element_type=jnp.float32)
    return (jax.nn.silu(pre_gate + lifted[0]) * (pre_up + lifted[1])).astype(jnp.bfloat16)


def share_partial(hidden_part, index_part, keep_part, down_tiles, squeeze, delta_last):
    row_count = hidden_part.shape[0]
    count_blocks = down_tiles.shape[0]
    model_width = delta_last.shape[1]
    tile_keep = keep_part.astype(jnp.bfloat16)[:, :, None, None]
    pieces = jnp.einsum(
        "rfh,fkhc->rfkc",
        hidden_part.reshape(row_count, count_blocks, 128),
        down_tiles * tile_keep,
        preferred_element_type=jnp.float32,
    )
    placed = (
        jnp.zeros((row_count, model_width // 128, 128), jnp.float32)
        .at[:, index_part.reshape(-1)]
        .add(pieces.reshape(row_count, -1, 128))
    )
    squeezed = jnp.dot(hidden_part, squeeze, preferred_element_type=jnp.float32).astype(
        jnp.bfloat16
    )
    return placed.reshape(row_count, model_width) + jnp.dot(
        squeezed, delta_last, preferred_element_type=jnp.float32
    )


def per_device(
    tokens,
    routes,
    route_weight,
    base_index,
    expert_mask,
    base_gate,
    base_up,
    base_down,
    delta_in,
    delta_gate_up,
    delta_down_in,
    delta_out,
):
    tok_count, model_width = tokens.shape
    choose = routes.shape[1]
    exp_size = lax.axis_size("exp")
    base_size = lax.axis_size("base")
    half_blocks = base_gate.shape[0]
    most_rows = min(tok_count, max(2, (tok_count * choose + exp_size - 1) // exp_size * 3 // 2))
    own_targets = place_rows(routes, exp_size, most_rows, 1, 0)
    offset = lax.axis_index("base") * half_blocks
    my_index = lax.dynamic_slice_in_dim(base_index, offset, half_blocks, 0)
    my_keep = lax.dynamic_slice_in_dim(expert_mask[0], offset, half_blocks, 0)
    pair_tokens, pair_routes = (
        lax.all_gather(tokens, "base", axis=0, tiled=True),
        lax.all_gather(routes.astype(jnp.bfloat16), "base", axis=0, tiled=True),
    )
    pair_routes = pair_routes.astype(jnp.int32)
    targets = jnp.concatenate(
        [
            place_rows(
                pair_routes[copy_index * tok_count : (copy_index + 1) * tok_count],
                exp_size,
                most_rows,
                base_size,
                copy_index,
            )
            for copy_index in range(base_size)
        ]
    )
    spread = spread_matrix(targets, exp_size * base_size * most_rows, choose)
    outgoing = jnp.dot(spread, pair_tokens, preferred_element_type=jnp.float32).astype(jnp.bfloat16)
    outgoing = outgoing.reshape(exp_size, base_size * most_rows, model_width)
    arrived = lax.all_to_all(outgoing, "exp", split_axis=0, concat_axis=0, tiled=True)
    incoming = arrived.reshape(-1, model_width)
    hidden = hidden_units(
        incoming, my_index, my_keep, base_gate, base_up, delta_in[0], delta_gate_up[0]
    )
    partial_value = share_partial(
        hidden, my_index, my_keep, base_down, delta_down_in[0], delta_out[0]
    )
    summed = lax.psum_scatter(
        partial_value.reshape(exp_size, base_size, most_rows, model_width).astype(jnp.bfloat16),
        "base",
        scatter_dimension=1,
        tiled=True,
    )
    results = summed.reshape(exp_size, most_rows, model_width)
    returned = lax.all_to_all(results, "exp", split_axis=0, concat_axis=0, tiled=True).reshape(
        exp_size * most_rows, model_width
    )
    gathered = returned[own_targets.reshape(tok_count, choose)]
    combined = jnp.sum(route_weight[:, :, None] * gathered.astype(jnp.float32), axis=1)
    return combined.astype(jnp.bfloat16)


def solution(mesh):
    small = mesh.shape["base"] == 1 and mesh.shape["exp"] == 16
    return jax.shard_map(
        per_device_fused if small else per_device,
        mesh=mesh,
        in_specs=(
            P(("groups", "exp", "base"), None),
            P(("groups", "exp", "base"), None),
            P(("groups", "exp", "base"), None),
            P(),
            P("exp", None, None),
            P("base", None, None, None),
            P("base", None, None, None),
            P("base", None, None, None),
            P("exp", None, None),
            P("exp", None, None, "base"),
            P("exp", "base", None),
            P("exp", None, None),
        ),
        out_specs=P(("groups", "exp", "base"), None),
        check_vma=False,
    )
```

```python
import functools

import jax
import jax.numpy as jnp
from jax import lax
from jax.experimental import pallas as pl
from jax.experimental.pallas import tpu as pltpu
from jax.sharding import PartitionSpec as P

LANES = 128


def fused_kernel(
    nz,
    gather_cuts,
    reduce_cuts,
    tokens_ref,
    routes_ref,
    choice_ref,
    index_ref,
    keep_ref,
    meta_ref,
    gate_hbm,
    up_hbm,
    down_hbm,
    first_hbm,
    lift_hbm,
    squeeze_hbm,
    last_hbm,
    out_ref,
    tok,
    columns,
    gate_v,
    up_v,
    down_v,
    first_v,
    lift_v,
    squeeze_v,
    last_v,
    hidden,
    segment,
    part,
    scale,
    from_core,
    from_x,
    from_low,
    from_high,
    to_x,
    to_z,
    acc,
    weight_sem,
    gz_recv,
    gx_recv,
    gc_recv,
    gup_send,
    gdown_send,
    gx_send,
    gc_send,
    rc_recv,
    rx_recv,
    rlow_recv,
    rhigh_recv,
    rc_send,
    rx_send,
    rz_send,
):
    rows, width = tokens_ref.shape
    blocks = width // LANES
    pairs = gate_v.shape[0]
    count_blocks = hidden.shape[0]
    per_block = pairs // count_blocks
    all_rows = tok.shape[0]
    me = lax.axis_index("exp")
    core = lax.rem(me, 2)
    x = lax.rem(me // 2, 2)
    z = me // 4

    def place(pz, px, pc):
        return (pz * 2 + px) * 2 + pc

    core_peer = place(z, x, 1 - core)
    x_peer = place(z, 1 - x, core)
    up_peer = me + 4
    down_peer = me - 4
    has_up = z < nz - 1
    has_down = z > 0

    def fetch(position, source, target):
        return pltpu.make_async_copy(source, target, weight_sem.at[position])

    fetches = [
        fetch(0, first_hbm, first_v),
        fetch(1, gate_hbm, gate_v),
        fetch(2, up_hbm, up_v),
        fetch(3, lift_hbm, lift_v),
        fetch(4, down_hbm, down_v),
        fetch(5, squeeze_hbm, squeeze_v),
        fetch(6, last_hbm, last_v),
    ]

    barrier = pltpu.get_barrier_semaphore()

    def greet(peer):
        pl.semaphore_signal(
            barrier, inc=1, device_id={"exp": peer}, device_id_type=pl.DeviceIdType.MESH
        )

    greet(core_peer)
    greet(x_peer)

    @pl.when(has_up)
    def _():
        greet(up_peer)

    @pl.when(has_down)
    def _():
        greet(down_peer)

    own_rows = pl.ds(pl.multiple_of(me * rows, rows), rows)
    tok[own_rows, :width] = tokens_ref[...]
    experts = 4 * nz
    lane = lax.broadcasted_iota(jnp.int32, (rows, LANES), 1)
    expert = lax.rem(lane, experts)
    weights = jnp.zeros((rows, LANES), jnp.float32)
    for k in range(routes_ref.shape[1]):
        named = routes_ref[:, k : k + 1] == expert
        weights = weights + jnp.where(named, choice_ref[:, k : k + 1], 0.0)
    weights = jnp.where(lane < 3 * experts, weights, 0.0)
    high = weights.astype(jnp.bfloat16)
    rest = weights - high.astype(jnp.float32)
    middle = rest.astype(jnp.bfloat16)
    low_part = rest - middle.astype(jnp.float32)
    tok[own_rows, width:] = jnp.where(
        lane < experts,
        high.astype(jnp.float32),
        jnp.where(lane < 2 * experts, middle.astype(jnp.float32), low_part),
    ).astype(jnp.bfloat16)

    degree = 2 + has_up.astype(jnp.int32) + has_down.astype(jnp.int32)
    pl.semaphore_wait(barrier, degree)

    def remote(source, target, send, recv, peer):
        return pltpu.make_async_remote_copy(
            src_ref=source,
            dst_ref=target,
            send_sem=send,
            recv_sem=recv,
            device_id={"exp": peer},
            device_id_type=pl.DeviceIdType.MESH,
        )

    all_blocks = blocks + 1
    edges = [(part * all_blocks // gather_cuts) * LANES for part in range(gather_cuts + 1)]
    gather_parts = range(gather_cuts)

    def block_of(pz, px, pc, cut):
        at = pl.ds(pl.multiple_of(place(pz, px, pc) * rows, rows), rows)
        return tok.at[at, pl.ds(edges[cut], edges[cut + 1] - edges[cut])]

    def g_up(pz, cut):
        b = block_of(pz, x, core, cut)
        return remote(b, b, gup_send.at[pz, cut], gz_recv.at[pz, cut], up_peer)

    def g_down(pz, cut):
        b = block_of(pz, x, core, cut)
        return remote(b, b, gdown_send.at[pz, cut], gz_recv.at[pz, cut], down_peer)

    def g_x(pz, px, cut):
        b = block_of(pz, px, core, cut)
        return remote(b, b, gx_send.at[pz, cut], gx_recv.at[pz, cut], x_peer)

    def g_core(pz, px, pc, cut):
        b = block_of(pz, px, pc, cut)
        return remote(b, b, gc_send.at[pz, px, cut], gc_recv.at[pz, px, cut], core_peer)

    def both_sides(distance, act):
        @pl.when(z >= distance)
        def _():
            act(z - distance, True)

        @pl.when(z + distance < nz)
        def _():
            act(z + distance, False)

    def spread_x(pz, cut):
        g_x(pz, x, cut).start()
        g_core(pz, x, core, cut).start()

    def pass_on(cut, pz, upward):
        if upward:
            g_up(pz, cut).wait_recv()

            @pl.when(has_up)
            def _():
                g_up(pz, cut).start()
        else:
            g_down(pz, cut).wait_recv()

            @pl.when(has_down)
            def _():
                g_down(pz, cut).start()
        spread_x(pz, cut)

    def cross(cut, pz, upward=True):
        g_x(pz, 1 - x, cut).wait_recv()
        g_core(pz, 1 - x, core, cut).start()

    def at_distance(distance, act, cut):
        if distance == 0:
            act(cut, z)
        else:
            both_sides(distance, functools.partial(act, cut))

    for cut in gather_parts:

        @pl.when(has_up)
        def _():
            g_up(z, cut).start()

        @pl.when(has_down)
        def _():
            g_down(z, cut).start()

        spread_x(z, cut)
    for one in fetches:
        one.start()
    half_rows = all_rows // 2
    own_half = z // (nz // 2)
    other_half = 1 - own_half

    def half_at(half):
        return pl.ds(pl.multiple_of(half * half_rows, half_rows), half_rows)

    def core_arrived(half):
        for step in range(nz // 2):
            for px in range(2):
                for cut in gather_parts:
                    g_core(half * (nz // 2) + step, px, 1 - core, cut).wait_recv()

    depth = 8 * LANES if blocks % 8 == 0 else LANES

    def keep_tile(value):
        some = jnp.full((16, LANES), value.astype(jnp.float32)).astype(jnp.bfloat16)
        return jnp.concatenate([some] * (LANES // 16), axis=0)

    def compute_hidden(half, meanwhile=None, midway=None):
        at_rows = half_at(half)
        sent = tok[at_rows, width:].astype(jnp.float32)
        lane = lax.broadcasted_iota(jnp.int32, sent.shape, 1)
        mine = jnp.logical_and(lax.rem(lane, experts) == me, lane < 3 * experts)
        column = jnp.sum(jnp.where(mine, sent, 0.0), axis=1, keepdims=True)
        scale[...] = jnp.broadcast_to(column, scale.shape)

        def column_step(d, carry):
            columns[d] = tok[at_rows, pl.ds(pl.multiple_of(d * LANES, LANES), LANES)]
            return carry

        lax.fori_loop(0, blocks, column_step, 0, unroll=4)

        def low_step(step, total):
            at = pl.ds(pl.multiple_of(step * depth, depth), depth)
            return total + jnp.dot(
                tok[at_rows, at], first_v[at, :], preferred_element_type=jnp.float32
            )

        low = lax.fori_loop(
            0, width // depth, low_step, jnp.zeros((half_rows, LANES), jnp.float32)
        ).astype(jnp.bfloat16)

        if meanwhile is not None:
            meanwhile()

        def hidden_step(f, carry):
            left, right = [], []
            for k in range(per_block):
                pair = f * per_block + k
                left.append(columns[index_ref[f, k]])
                keep = keep_tile(keep_ref[f, k])
                right.append(jnp.concatenate([gate_v[pair] * keep, up_v[pair] * keep], axis=1))
            units = pl.ds(pl.multiple_of(f * LANES, LANES), LANES)
            left.append(low)
            right.append(jnp.concatenate([lift_v[0, :, units], lift_v[1, :, units]], axis=1))
            both = jnp.dot(
                jnp.concatenate(left, axis=1),
                jnp.concatenate(right, axis=0),
                preferred_element_type=jnp.float32,
            )
            gate, up = both[:, :LANES], both[:, LANES:]
            hidden[f] = (gate / (1.0 + jnp.exp(-gate)) * up).astype(jnp.bfloat16)
            return carry

        if midway is None:
            lax.fori_loop(0, count_blocks, hidden_step, 0, unroll=2)
        else:
            lax.fori_loop(0, count_blocks // 2, hidden_step, 0, unroll=2)
            midway()
            lax.fori_loop(count_blocks // 2, count_blocks, hidden_step, 0, unroll=2)

    def compute_part(half, midway=None):
        at_rows = half_at(half)

        def squeeze_step(f, total):
            at = pl.ds(pl.multiple_of(f * LANES, LANES), LANES)
            return total + jnp.dot(hidden[f], squeeze_v[at, :], preferred_element_type=jnp.float32)

        squeezed = lax.fori_loop(
            0, count_blocks, squeeze_step, jnp.zeros((half_rows, LANES), jnp.float32), unroll=8
        ).astype(jnp.bfloat16)

        def down_step(step, total):
            pair = meta_ref[0, step]
            f = meta_ref[1, step]
            tile = down_v[pair] * keep_tile(keep_ref[f, pair - f * per_block])
            again = meta_ref[2, step].astype(jnp.float32)
            total = total * again + jnp.dot(
                hidden[f], tile, preferred_element_type=jnp.float32
            )
            segment[step] = total
            return total

        lax.fori_loop(
            0, pairs, down_step, jnp.zeros((half_rows, LANES), jnp.float32), unroll=8
        )

        if midway is not None:
            midway()

        def output_step(d, carry):
            at = pl.ds(pl.multiple_of(d * LANES, LANES), LANES)
            value = jnp.dot(squeezed, last_v[:, at], preferred_element_type=jnp.float32)
            value = value + segment[meta_ref[3, d]] * meta_ref[4, d].astype(jnp.float32)
            value = value.astype(jnp.bfloat16).astype(jnp.float32) * scale[...]
            part[at_rows, at] = value.astype(jnp.bfloat16)
            return carry

        lax.fori_loop(0, blocks, output_step, 0, unroll=4)

    for distance in range(1, nz - 1):
        for cut in gather_parts:
            at_distance(distance, pass_on, cut)
            at_distance(distance - 1, cross, cut)
    core_arrived(own_half)
    for one in fetches[:4]:
        one.wait()


    def forward(cut):
        at_distance(nz - 1, pass_on, cut)
        at_distance(nz - 2, cross, cut)

    def forward_early():
        for cut in range(gather_cuts - 1):
            forward(cut)

    compute_hidden(own_half, None, forward_early)
    forward(gather_cuts - 1)
    for one in fetches[4:]:
        one.wait()
    compute_part(own_half, lambda: at_distance(nz - 1, cross, 0))

    def part_of(pz, px, pc):
        return part.at[pl.ds(pl.multiple_of(place(pz, px, pc) * rows, rows), rows)]

    def r_core(pz, px):
        return remote(
            part_of(pz, px, 1 - core),
            from_core.at[pz, px],
            rc_send.at[pz, px],
            rc_recv.at[pz, px],
            core_peer,
        )

    step_width = width // reduce_cuts
    reduce_parts = range(reduce_cuts)

    def columns_of(cut):
        return pl.ds(cut * step_width, step_width)

    def r_x(pz, cut):
        at = columns_of(cut)
        return remote(
            to_x.at[pz, :, at],
            from_x.at[pz, :, at],
            rx_send.at[pz, cut],
            rx_recv.at[pz, cut],
            x_peer,
        )

    def r_up(pz, cut):
        at = columns_of(cut)
        return remote(
            to_z.at[pz, :, at],
            from_low.at[pz, :, at],
            rz_send.at[pz, cut],
            rlow_recv.at[pz, cut],
            up_peer,
        )

    def r_down(pz, cut):
        at = columns_of(cut)
        return remote(
            to_z.at[pz, :, at],
            from_high.at[pz, :, at],
            rz_send.at[pz, cut],
            rhigh_recv.at[pz, cut],
            down_peer,
        )

    def wide(value):
        return value.astype(jnp.float32)

    def core_start(pz, px):
        r_core(pz, px).start()

    mate = own_half * nz + nz // 2 - 1 - z
    toward = 1 - 2 * own_half
    near = jnp.where(own_half == 0, nz // 2, nz // 2 - 1)
    far = near + toward * (nz // 2 - 1)
    at_end = jnp.logical_or(z == 0, z == nz - 1)

    def part_at(pz, px, cut):
        at = pl.ds(pl.multiple_of(place(pz, px, core) * rows, rows), rows)
        return wide(part[at, columns_of(cut)])

    def x_start(pz):
        r_core(pz, 1 - x).wait_recv()
        for cut in reduce_parts:
            at = columns_of(cut)
            total = part_at(pz, 1 - x, cut) + wide(from_core[pz, 1 - x, :, at])
            to_x[pz, :, at] = total.astype(jnp.bfloat16)
            r_x(pz, cut).start()

    def local_sum(pz, cut):
        r_x(pz, cut).wait_recv()
        at = columns_of(cut)
        total = part_at(pz, x, cut) + wide(from_core[pz, x, :, at])
        return total + wide(from_x[pz, :, at])

    def z_step(pz):
        r_core(pz, x).wait_recv()
        for cut in reduce_parts:
            at = columns_of(cut)
            acc[:, at] = local_sum(pz, cut)

            @pl.when(pz < z)
            def _():
                @pl.when(has_up)
                def _():
                    r_down(pz, cut).wait_recv()
                    acc[:, at] += wide(from_high[pz, :, at])

                to_z[pz, :, at] = acc[:, at].astype(jnp.bfloat16)
                r_down(pz, cut).start()

            @pl.when(pz > z)
            def _():
                @pl.when(has_down)
                def _():
                    r_up(pz, cut).wait_recv()
                    acc[:, at] += wide(from_low[pz, :, at])

                to_z[pz, :, at] = acc[:, at].astype(jnp.bfloat16)
                r_up(pz, cut).start()

    for px in (1 - x, x):
        core_start(mate, px)
        core_start(z, px)

    def near_sums():
        x_start(mate)
        x_start(z)

    for cut in range(1, gather_cuts):
        at_distance(nz - 1, cross, cut)
    core_arrived(other_half)
    compute_hidden(other_half, near_sums)
    compute_part(other_half)
    for px in (1 - x, x):
        core_start(far, px)
        core_start(near, px)

    x_start(far)
    x_start(near)

    @pl.when(at_end)
    def _():
        z_step(mate)

    z_step(far)

    @pl.when(jnp.logical_not(at_end))
    def _():
        z_step(mate)

    z_step(near)
    r_core(z, x).wait_recv()
    for cut in reduce_parts:
        at = columns_of(cut)
        acc[:, at] = local_sum(z, cut)

        @pl.when(has_up)
        def _():
            r_down(z, cut).wait_recv()
            acc[:, at] += wide(from_high[z, :, at])

        @pl.when(has_down)
        def _():
            r_up(z, cut).wait_recv()
            acc[:, at] += wide(from_low[z, :, at])

        out_ref[:, at] = acc[:, at].astype(jnp.bfloat16)

    for pz in range(nz):
        for px in range(2):
            r_core(pz, px).wait_send()
        for cut in reduce_parts:
            r_x(pz, cut).wait_send()

            @pl.when(pz != z)
            def _():
                r_up(pz, cut).wait_send()

    for pz in range(nz):
        for cut in gather_parts:

            @pl.when(jnp.logical_and(has_up, pz <= z))
            def _():
                g_up(pz, cut).wait_send()

            @pl.when(jnp.logical_and(has_down, pz >= z))
            def _():
                g_down(pz, cut).wait_send()

            g_x(pz, x, cut).wait_send()
            for px in range(2):
                g_core(pz, px, core, cut).wait_send()


def tile_plan(base_index, blocks):
    flat = base_index.reshape(-1)
    pairs = flat.shape[0]
    place = jnp.arange(pairs, dtype=jnp.int32)
    ahead = (flat[:, None] < flat[None, :]) | (
        (flat[:, None] == flat[None, :]) & (place[:, None] < place[None, :])
    )
    rank = jnp.sum(ahead.astype(jnp.int32), axis=0)
    chosen = (rank[:, None] == place[None, :]).astype(jnp.int32)
    order = jnp.sum(chosen * place[:, None], axis=0)
    sorted_block = jnp.sum(chosen * flat[:, None], axis=0)
    again = jnp.concatenate(
        [jnp.zeros((1,), jnp.int32), (sorted_block[1:] == sorted_block[:-1]).astype(jnp.int32)]
    )
    block = jnp.arange(blocks, dtype=jnp.int32)
    upto = jnp.sum((flat[:, None] <= block[None, :]).astype(jnp.int32), axis=0)
    used = jnp.any(flat[:, None] == block[None, :], axis=0).astype(jnp.int32)
    size = max(pairs, blocks)

    def row(values):
        return jnp.pad(values, (0, size - values.shape[0]))

    return jnp.stack(
        [
            row(order),
            row(order // base_index.shape[1]),
            row(again),
            row(jnp.maximum(upto - 1, 0)),
            row(used),
        ]
    )


def per_device_fused(
    tokens,
    routes,
    route_weight,
    base_index,
    expert_mask,
    base_gate,
    base_up,
    base_down,
    delta_in,
    delta_gate_up,
    delta_down_in,
    delta_out,
):
    rows, width = tokens.shape
    experts = lax.axis_size("exp")
    nz = experts // 4
    blocks = width // LANES
    count_blocks, per_block = base_index.shape
    pairs = count_blocks * per_block
    all_rows = rows * experts
    meta = tile_plan(base_index, blocks)
    lift = delta_gate_up[0]
    units = lift.shape[2]
    bf16, f32 = jnp.bfloat16, jnp.float32
    vmem, smem, anywhere = (
        pl.BlockSpec(memory_space=space) for space in (pltpu.VMEM, pltpu.SMEM, pl.ANY)
    )
    dma = pltpu.SemaphoreType.DMA
    gather_cuts = 2
    reduce_cuts = 4 if blocks % 4 == 0 else 1
    return pl.pallas_call(
        functools.partial(fused_kernel, nz, gather_cuts, reduce_cuts),
        out_shape=jax.ShapeDtypeStruct((rows, width), bf16),
        in_specs=[vmem, vmem, vmem, smem, smem, smem] + [anywhere] * 7,
        out_specs=vmem,
        scratch_shapes=[
            pltpu.VMEM((all_rows, width + LANES), bf16),
            pltpu.VMEM((blocks, all_rows // 2, LANES), bf16),
            pltpu.VMEM((pairs, LANES, LANES), bf16),
            pltpu.VMEM((pairs, LANES, LANES), bf16),
            pltpu.VMEM((pairs, LANES, LANES), bf16),
            pltpu.VMEM((width, LANES), bf16),
            pltpu.VMEM((2, LANES, units), bf16),
            pltpu.VMEM((units, LANES), bf16),
            pltpu.VMEM((LANES, width), bf16),
            pltpu.VMEM((count_blocks, all_rows // 2, LANES), bf16),
            pltpu.VMEM((pairs, all_rows // 2, LANES), f32),
            pltpu.VMEM((all_rows, width), bf16),
            pltpu.VMEM((all_rows // 2, LANES), f32),
            pltpu.VMEM((nz, 2, rows, width), bf16),
            pltpu.VMEM((nz, rows, width), bf16),
            pltpu.VMEM((nz, rows, width), bf16),
            pltpu.VMEM((nz, rows, width), bf16),
            pltpu.VMEM((nz, rows, width), bf16),
            pltpu.VMEM((nz, rows, width), bf16),
            pltpu.VMEM((rows, width), f32),
            dma((7,)),
            dma((nz, gather_cuts)),
            dma((nz, gather_cuts)),
            dma((nz, 2, gather_cuts)),
            dma((nz, gather_cuts)),
            dma((nz, gather_cuts)),
            dma((nz, gather_cuts)),
            dma((nz, 2, gather_cuts)),
            dma((nz, 2)),
            dma((nz, reduce_cuts)),
            dma((nz, reduce_cuts)),
            dma((nz, reduce_cuts)),
            dma((nz, 2)),
            dma((nz, reduce_cuts)),
            dma((nz, reduce_cuts)),
        ],
        compiler_params=pltpu.CompilerParams(
            collective_id=0, has_side_effects=True, vmem_limit_bytes=60 << 20
        ),
        name="expert_layer",
    )(
        tokens,
        routes,
        route_weight,
        base_index,
        expert_mask[0],
        meta,
        base_gate.reshape(pairs, LANES, LANES),
        base_up.reshape(pairs, LANES, LANES),
        base_down.reshape(pairs, LANES, LANES),
        delta_in[0],
        lift,
        delta_down_in[0],
        delta_out[0],
    )


def place_rows(route_block, experts, most_rows, copies, copy_index):
    flat_routes = route_block.reshape(-1)
    onehot = (flat_routes[:, None] == jnp.arange(experts, dtype=jnp.int32)[None, :]).astype(
        jnp.int32
    )
    before = jnp.cumsum(onehot, axis=0) - onehot
    slot_index = jnp.sum(before * onehot, axis=1)
    return (flat_routes * copies + copy_index) * most_rows + slot_index


def spread_matrix(targets, slot_count, choose):
    matches = targets[None, :] == jnp.arange(slot_count, dtype=jnp.int32)[:, None]
    return jnp.any(matches.reshape(slot_count, -1, choose), axis=2).astype(jnp.bfloat16)


def hidden_units(incoming, index_part, keep_part, gate_tiles, up_tiles, delta_first, lift):
    row_count, model_width = incoming.shape
    blocks = model_width // 128
    count_blocks, per_block = index_part.shape
    picked = jnp.take(incoming.reshape(row_count, blocks, 128), index_part.reshape(-1), axis=1)
    picked = picked.reshape(row_count, count_blocks, per_block, 128)
    tile_keep = keep_part.astype(jnp.bfloat16)[:, :, None, None]
    pre_gate = jnp.einsum(
        "rfkc,fkch->rfh", picked, gate_tiles * tile_keep, preferred_element_type=jnp.float32
    ).reshape(row_count, -1)
    pre_up = jnp.einsum(
        "rfkc,fkch->rfh", picked, up_tiles * tile_keep, preferred_element_type=jnp.float32
    ).reshape(row_count, -1)
    lowrank = jnp.dot(incoming, delta_first, preferred_element_type=jnp.float32).astype(
        jnp.bfloat16
    )
    lifted = jnp.einsum("rq,gqh->grh", lowrank, lift, preferred_element_type=jnp.float32)
    return (jax.nn.silu(pre_gate + lifted[0]) * (pre_up + lifted[1])).astype(jnp.bfloat16)


def share_partial(hidden_part, index_part, keep_part, down_tiles, squeeze, delta_last):
    row_count = hidden_part.shape[0]
    count_blocks = down_tiles.shape[0]
    model_width = delta_last.shape[1]
    tile_keep = keep_part.astype(jnp.bfloat16)[:, :, None, None]
    pieces = jnp.einsum(
        "rfh,fkhc->rfkc",
        hidden_part.reshape(row_count, count_blocks, 128),
        down_tiles * tile_keep,
        preferred_element_type=jnp.float32,
    )
    placed = (
        jnp.zeros((row_count, model_width // 128, 128), jnp.float32)
        .at[:, index_part.reshape(-1)]
        .add(pieces.reshape(row_count, -1, 128))
    )
    squeezed = jnp.dot(hidden_part, squeeze, preferred_element_type=jnp.float32).astype(
        jnp.bfloat16
    )
    return placed.reshape(row_count, model_width) + jnp.dot(
        squeezed, delta_last, preferred_element_type=jnp.float32
    )


def per_device(
    tokens,
    routes,
    route_weight,
    base_index,
    expert_mask,
    base_gate,
    base_up,
    base_down,
    delta_in,
    delta_gate_up,
    delta_down_in,
    delta_out,
):
    tok_count, model_width = tokens.shape
    choose = routes.shape[1]
    exp_size = lax.axis_size("exp")
    base_size = lax.axis_size("base")
    half_blocks = base_gate.shape[0]
    most_rows = min(tok_count, max(2, (tok_count * choose + exp_size - 1) // exp_size * 3 // 2))
    own_targets = place_rows(routes, exp_size, most_rows, 1, 0)
    offset = lax.axis_index("base") * half_blocks
    my_index = lax.dynamic_slice_in_dim(base_index, offset, half_blocks, 0)
    my_keep = lax.dynamic_slice_in_dim(expert_mask[0], offset, half_blocks, 0)
    pair_tokens, pair_routes = (
        lax.all_gather(tokens, "base", axis=0, tiled=True),
        lax.all_gather(routes.astype(jnp.bfloat16), "base", axis=0, tiled=True),
    )
    pair_routes = pair_routes.astype(jnp.int32)
    targets = jnp.concatenate(
        [
            place_rows(
                pair_routes[copy_index * tok_count : (copy_index + 1) * tok_count],
                exp_size,
                most_rows,
                base_size,
                copy_index,
            )
            for copy_index in range(base_size)
        ]
    )
    spread = spread_matrix(targets, exp_size * base_size * most_rows, choose)
    outgoing = jnp.dot(spread, pair_tokens, preferred_element_type=jnp.float32).astype(jnp.bfloat16)
    outgoing = outgoing.reshape(exp_size, base_size * most_rows, model_width)
    arrived = lax.all_to_all(outgoing, "exp", split_axis=0, concat_axis=0, tiled=True)
    incoming = arrived.reshape(-1, model_width)
    hidden = hidden_units(
        incoming, my_index, my_keep, base_gate, base_up, delta_in[0], delta_gate_up[0]
    )
    partial_value = share_partial(
        hidden, my_index, my_keep, base_down, delta_down_in[0], delta_out[0]
    )
    summed = lax.psum_scatter(
        partial_value.reshape(exp_size, base_size, most_rows, model_width).astype(jnp.bfloat16),
        "base",
        scatter_dimension=1,
        tiled=True,
    )
    results = summed.reshape(exp_size, most_rows, model_width)
    returned = lax.all_to_all(results, "exp", split_axis=0, concat_axis=0, tiled=True).reshape(
        exp_size * most_rows, model_width
    )
    gathered = returned[own_targets.reshape(tok_count, choose)]
    combined = jnp.sum(route_weight[:, :, None] * gathered.astype(jnp.float32), axis=1)
    return combined.astype(jnp.bfloat16)


def solution(mesh):
    small = mesh.shape["base"] == 1 and mesh.shape["exp"] == 16
    return jax.shard_map(
        per_device_fused if small else per_device,
        mesh=mesh,
        in_specs=(
            P(("groups", "exp", "base"), None),
            P(("groups", "exp", "base"), None),
            P(("groups", "exp", "base"), None),
            P(),
            P("exp", None, None),
            P("base", None, None, None),
            P("base", None, None, None),
            P("base", None, None, None),
            P("exp", None, None),
            P("exp", None, None, "base"),
            P("exp", "base", None),
            P("exp", None, None),
        ),
        out_specs=P(("groups", "exp", "base"), None),
        check_vma=False,
    )
```

```python
import functools

import jax
import jax.numpy as jnp
from jax import lax
from jax.experimental import pallas as pl
from jax.experimental.pallas import tpu as pltpu
from jax.sharding import PartitionSpec as P

LANES = 128


def fused_kernel(
    nz,
    gather_cuts,
    reduce_cuts,
    tokens_ref,
    weight_ref,
    index_ref,
    keep_ref,
    meta_ref,
    gate_hbm,
    up_hbm,
    down_hbm,
    first_hbm,
    lift_hbm,
    squeeze_hbm,
    last_hbm,
    out_ref,
    tok,
    columns,
    gate_v,
    up_v,
    down_v,
    first_v,
    lift_v,
    squeeze_v,
    last_v,
    hidden,
    segment,
    part,
    scale,
    from_core,
    from_x,
    from_low,
    from_high,
    to_x,
    to_z,
    acc,
    weight_sem,
    gz_recv,
    gx_recv,
    gc_recv,
    gup_send,
    gdown_send,
    gx_send,
    gc_send,
    rc_recv,
    rx_recv,
    rlow_recv,
    rhigh_recv,
    rc_send,
    rx_send,
    rz_send,
):
    rows, width = tokens_ref.shape
    blocks = width // LANES
    pairs = gate_v.shape[0]
    count_blocks = hidden.shape[0]
    per_block = pairs // count_blocks
    all_rows = tok.shape[0]
    me = lax.axis_index("exp")
    core = lax.rem(me, 2)
    x = lax.rem(me // 2, 2)
    z = me // 4

    def place(pz, px, pc):
        return (pz * 2 + px) * 2 + pc

    core_peer = place(z, x, 1 - core)
    x_peer = place(z, 1 - x, core)
    up_peer = me + 4
    down_peer = me - 4
    has_up = z < nz - 1
    has_down = z > 0

    def fetch(position, source, target):
        return pltpu.make_async_copy(source, target, weight_sem.at[position])

    fetches = [
        fetch(0, first_hbm, first_v),
        fetch(1, gate_hbm, gate_v),
        fetch(2, up_hbm, up_v),
        fetch(3, lift_hbm, lift_v),
        fetch(4, down_hbm, down_v),
        fetch(5, squeeze_hbm, squeeze_v),
        fetch(6, last_hbm, last_v),
    ]

    barrier = pltpu.get_barrier_semaphore()

    def greet(peer):
        pl.semaphore_signal(
            barrier, inc=1, device_id={"exp": peer}, device_id_type=pl.DeviceIdType.MESH
        )

    greet(core_peer)
    greet(x_peer)

    @pl.when(has_up)
    def _():
        greet(up_peer)

    @pl.when(has_down)
    def _():
        greet(down_peer)

    own_rows = pl.ds(pl.multiple_of(me * rows, rows), rows)
    tok[own_rows, :width] = tokens_ref[...]
    weights = weight_ref[...]
    lane = lax.broadcasted_iota(jnp.int32, weights.shape, 1)
    high = weights.astype(jnp.bfloat16)
    rest = weights - high.astype(jnp.float32)
    middle = rest.astype(jnp.bfloat16)
    low_part = rest - middle.astype(jnp.float32)
    experts = 4 * nz
    tok[own_rows, width:] = jnp.where(
        lane < experts,
        high.astype(jnp.float32),
        jnp.where(lane < 2 * experts, middle.astype(jnp.float32), low_part),
    ).astype(jnp.bfloat16)

    degree = 2 + has_up.astype(jnp.int32) + has_down.astype(jnp.int32)
    pl.semaphore_wait(barrier, degree)

    def remote(source, target, send, recv, peer):
        return pltpu.make_async_remote_copy(
            src_ref=source,
            dst_ref=target,
            send_sem=send,
            recv_sem=recv,
            device_id={"exp": peer},
            device_id_type=pl.DeviceIdType.MESH,
        )

    all_blocks = blocks + 1
    edges = [(part * all_blocks // gather_cuts) * LANES for part in range(gather_cuts + 1)]
    gather_parts = range(gather_cuts)

    def block_of(pz, px, pc, cut):
        at = pl.ds(pl.multiple_of(place(pz, px, pc) * rows, rows), rows)
        return tok.at[at, pl.ds(edges[cut], edges[cut + 1] - edges[cut])]

    def g_up(pz, cut):
        b = block_of(pz, x, core, cut)
        return remote(b, b, gup_send.at[pz, cut], gz_recv.at[pz, cut], up_peer)

    def g_down(pz, cut):
        b = block_of(pz, x, core, cut)
        return remote(b, b, gdown_send.at[pz, cut], gz_recv.at[pz, cut], down_peer)

    def g_x(pz, px, cut):
        b = block_of(pz, px, core, cut)
        return remote(b, b, gx_send.at[pz, cut], gx_recv.at[pz, cut], x_peer)

    def g_core(pz, px, pc, cut):
        b = block_of(pz, px, pc, cut)
        return remote(b, b, gc_send.at[pz, px, cut], gc_recv.at[pz, px, cut], core_peer)

    def both_sides(distance, act):
        @pl.when(z >= distance)
        def _():
            act(z - distance, True)

        @pl.when(z + distance < nz)
        def _():
            act(z + distance, False)

    def spread_x(pz, cut):
        g_x(pz, x, cut).start()
        g_core(pz, x, core, cut).start()

    def pass_on(cut, pz, upward):
        if upward:
            g_up(pz, cut).wait_recv()

            @pl.when(has_up)
            def _():
                g_up(pz, cut).start()
        else:
            g_down(pz, cut).wait_recv()

            @pl.when(has_down)
            def _():
                g_down(pz, cut).start()
        spread_x(pz, cut)

    def cross(cut, pz, upward=True):
        g_x(pz, 1 - x, cut).wait_recv()
        g_core(pz, 1 - x, core, cut).start()

    def at_distance(distance, act, cut):
        if distance == 0:
            act(cut, z)
        else:
            both_sides(distance, functools.partial(act, cut))

    for cut in gather_parts:

        @pl.when(has_up)
        def _():
            g_up(z, cut).start()

        @pl.when(has_down)
        def _():
            g_down(z, cut).start()

        spread_x(z, cut)
    for one in fetches:
        one.start()
    half_rows = all_rows // 2
    own_half = z // (nz // 2)
    other_half = 1 - own_half

    def half_at(half):
        return pl.ds(pl.multiple_of(half * half_rows, half_rows), half_rows)

    def core_arrived(half):
        for step in range(nz // 2):
            for px in range(2):
                for cut in gather_parts:
                    g_core(half * (nz // 2) + step, px, 1 - core, cut).wait_recv()

    depth = 8 * LANES if blocks % 8 == 0 else LANES

    def keep_tile(value):
        some = jnp.full((16, LANES), value.astype(jnp.float32)).astype(jnp.bfloat16)
        return jnp.concatenate([some] * (LANES // 16), axis=0)

    def compute_hidden(half, meanwhile=None):
        at_rows = half_at(half)
        sent = tok[at_rows, width:].astype(jnp.float32)
        lane = lax.broadcasted_iota(jnp.int32, sent.shape, 1)
        mine = jnp.logical_and(lax.rem(lane, experts) == me, lane < 3 * experts)
        column = jnp.sum(jnp.where(mine, sent, 0.0), axis=1, keepdims=True)
        scale[...] = jnp.broadcast_to(column, scale.shape)

        def column_step(d, carry):
            columns[d] = tok[at_rows, pl.ds(pl.multiple_of(d * LANES, LANES), LANES)]
            return carry

        lax.fori_loop(0, blocks, column_step, 0, unroll=4)

        def low_step(step, total):
            at = pl.ds(pl.multiple_of(step * depth, depth), depth)
            return total + jnp.dot(
                tok[at_rows, at], first_v[at, :], preferred_element_type=jnp.float32
            )

        low = lax.fori_loop(
            0, width // depth, low_step, jnp.zeros((half_rows, LANES), jnp.float32)
        ).astype(jnp.bfloat16)

        if meanwhile is not None:
            meanwhile()

        def hidden_step(f, carry):
            left, right = [], []
            for k in range(per_block):
                pair = f * per_block + k
                left.append(columns[index_ref[k, f]])
                keep = keep_tile(keep_ref[k, f])
                right.append(jnp.concatenate([gate_v[pair] * keep, up_v[pair] * keep], axis=1))
            units = pl.ds(pl.multiple_of(f * LANES, LANES), LANES)
            left.append(low)
            right.append(jnp.concatenate([lift_v[0, :, units], lift_v[1, :, units]], axis=1))
            both = jnp.dot(
                jnp.concatenate(left, axis=1),
                jnp.concatenate(right, axis=0),
                preferred_element_type=jnp.float32,
            )
            gate, up = both[:, :LANES], both[:, LANES:]
            hidden[f] = (gate / (1.0 + jnp.exp(-gate)) * up).astype(jnp.bfloat16)
            return carry

        lax.fori_loop(0, count_blocks, hidden_step, 0, unroll=2)

    def compute_part(half):
        at_rows = half_at(half)

        def squeeze_step(f, total):
            at = pl.ds(pl.multiple_of(f * LANES, LANES), LANES)
            return total + jnp.dot(hidden[f], squeeze_v[at, :], preferred_element_type=jnp.float32)

        squeezed = lax.fori_loop(
            0, count_blocks, squeeze_step, jnp.zeros((half_rows, LANES), jnp.float32), unroll=8
        ).astype(jnp.bfloat16)

        def down_step(step, total):
            pair = meta_ref[0, step]
            f = meta_ref[1, step]
            tile = down_v[pair] * keep_tile(keep_ref[pair - f * per_block, f])
            again = meta_ref[2, step].astype(jnp.float32)
            total = total * again + jnp.dot(
                hidden[f], tile, preferred_element_type=jnp.float32
            )
            segment[step] = total
            return total

        lax.fori_loop(
            0, pairs, down_step, jnp.zeros((half_rows, LANES), jnp.float32), unroll=8
        )

        def output_step(d, carry):
            at = pl.ds(pl.multiple_of(d * LANES, LANES), LANES)
            value = jnp.dot(squeezed, last_v[:, at], preferred_element_type=jnp.float32)
            value = value + segment[meta_ref[3, d]] * meta_ref[4, d].astype(jnp.float32)
            value = value.astype(jnp.bfloat16).astype(jnp.float32) * scale[...]
            part[at_rows, at] = value.astype(jnp.bfloat16)
            return carry

        lax.fori_loop(0, blocks, output_step, 0, unroll=4)

    for distance in range(1, nz - 1):
        for cut in gather_parts:
            at_distance(distance, pass_on, cut)
            at_distance(distance - 1, cross, cut)
    core_arrived(own_half)
    for one in fetches[:4]:
        one.wait()

    compute_hidden(own_half)
    for cut in gather_parts:
        at_distance(nz - 1, pass_on, cut)
        at_distance(nz - 2, cross, cut)
    for one in fetches[4:]:
        one.wait()
    compute_part(own_half)
    for cut in gather_parts:
        at_distance(nz - 1, cross, cut)
    core_arrived(other_half)

    def part_of(pz, px, pc):
        return part.at[pl.ds(pl.multiple_of(place(pz, px, pc) * rows, rows), rows)]

    def r_core(pz, px):
        return remote(
            part_of(pz, px, 1 - core),
            from_core.at[pz, px],
            rc_send.at[pz, px],
            rc_recv.at[pz, px],
            core_peer,
        )

    step_width = width // reduce_cuts
    reduce_parts = range(reduce_cuts)

    def columns_of(cut):
        return pl.ds(cut * step_width, step_width)

    def r_x(pz, cut):
        at = columns_of(cut)
        return remote(
            to_x.at[pz, :, at],
            from_x.at[pz, :, at],
            rx_send.at[pz, cut],
            rx_recv.at[pz, cut],
            x_peer,
        )

    def r_up(pz, cut):
        at = columns_of(cut)
        return remote(
            to_z.at[pz, :, at],
            from_low.at[pz, :, at],
            rz_send.at[pz, cut],
            rlow_recv.at[pz, cut],
            up_peer,
        )

    def r_down(pz, cut):
        at = columns_of(cut)
        return remote(
            to_z.at[pz, :, at],
            from_high.at[pz, :, at],
            rz_send.at[pz, cut],
            rhigh_recv.at[pz, cut],
            down_peer,
        )

    def wide(value):
        return value.astype(jnp.float32)

    def core_start(pz, px):
        r_core(pz, px).start()

    mate = own_half * nz + nz // 2 - 1 - z
    toward = 1 - 2 * own_half
    near = jnp.where(own_half == 0, nz // 2, nz // 2 - 1)
    far = near + toward * (nz // 2 - 1)
    at_end = jnp.logical_or(z == 0, z == nz - 1)

    def part_at(pz, px, cut):
        at = pl.ds(pl.multiple_of(place(pz, px, core) * rows, rows), rows)
        return wide(part[at, columns_of(cut)])

    def x_start(pz):
        r_core(pz, 1 - x).wait_recv()
        for cut in reduce_parts:
            at = columns_of(cut)
            total = part_at(pz, 1 - x, cut) + wide(from_core[pz, 1 - x, :, at])
            to_x[pz, :, at] = total.astype(jnp.bfloat16)
            r_x(pz, cut).start()

    def local_sum(pz, cut):
        r_x(pz, cut).wait_recv()
        at = columns_of(cut)
        total = part_at(pz, x, cut) + wide(from_core[pz, x, :, at])
        return total + wide(from_x[pz, :, at])

    def z_step(pz):
        r_core(pz, x).wait_recv()
        for cut in reduce_parts:
            at = columns_of(cut)
            acc[:, at] = local_sum(pz, cut)

            @pl.when(pz < z)
            def _():
                @pl.when(has_up)
                def _():
                    r_down(pz, cut).wait_recv()
                    acc[:, at] += wide(from_high[pz, :, at])

                to_z[pz, :, at] = acc[:, at].astype(jnp.bfloat16)
                r_down(pz, cut).start()

            @pl.when(pz > z)
            def _():
                @pl.when(has_down)
                def _():
                    r_up(pz, cut).wait_recv()
                    acc[:, at] += wide(from_low[pz, :, at])

                to_z[pz, :, at] = acc[:, at].astype(jnp.bfloat16)
                r_up(pz, cut).start()

    for px in (1 - x, x):
        core_start(mate, px)
        core_start(z, px)

    def near_sums():
        x_start(mate)
        x_start(z)

    compute_hidden(other_half, near_sums)
    compute_part(other_half)
    for px in (1 - x, x):
        core_start(far, px)
        core_start(near, px)

    x_start(far)
    x_start(near)

    @pl.when(at_end)
    def _():
        z_step(mate)

    z_step(far)

    @pl.when(jnp.logical_not(at_end))
    def _():
        z_step(mate)

    z_step(near)
    r_core(z, x).wait_recv()
    for cut in reduce_parts:
        at = columns_of(cut)
        acc[:, at] = local_sum(z, cut)

        @pl.when(has_up)
        def _():
            r_down(z, cut).wait_recv()
            acc[:, at] += wide(from_high[z, :, at])

        @pl.when(has_down)
        def _():
            r_up(z, cut).wait_recv()
            acc[:, at] += wide(from_low[z, :, at])

        out_ref[:, at] = acc[:, at].astype(jnp.bfloat16)

    for pz in range(nz):
        for px in range(2):
            r_core(pz, px).wait_send()
        for cut in reduce_parts:
            r_x(pz, cut).wait_send()

            @pl.when(pz != z)
            def _():
                r_up(pz, cut).wait_send()

    for pz in range(nz):
        for cut in gather_parts:

            @pl.when(jnp.logical_and(has_up, pz <= z))
            def _():
                g_up(pz, cut).wait_send()

            @pl.when(jnp.logical_and(has_down, pz >= z))
            def _():
                g_down(pz, cut).wait_send()

            g_x(pz, x, cut).wait_send()
            for px in range(2):
                g_core(pz, px, core, cut).wait_send()


def tile_plan(index_rows, blocks):
    per_block, count_blocks = index_rows.shape
    flat = index_rows.reshape(-1)
    pairs = flat.shape[0]
    place = jnp.arange(pairs, dtype=jnp.int32)
    ahead = (flat[:, None] < flat[None, :]) | (
        (flat[:, None] == flat[None, :]) & (place[:, None] < place[None, :])
    )
    rank = jnp.sum(ahead.astype(jnp.int32), axis=0)
    chosen = (rank[:, None] == place[None, :]).astype(jnp.int32)
    unit_block = place % count_blocks
    stored = unit_block * per_block + place // count_blocks
    order = jnp.sum(chosen * stored[:, None], axis=0)
    order_block = jnp.sum(chosen * unit_block[:, None], axis=0)
    sorted_block = jnp.sum(chosen * flat[:, None], axis=0)
    again = jnp.concatenate(
        [jnp.zeros((1,), jnp.int32), (sorted_block[1:] == sorted_block[:-1]).astype(jnp.int32)]
    )
    block = jnp.arange(blocks, dtype=jnp.int32)
    upto = jnp.sum((flat[:, None] <= block[None, :]).astype(jnp.int32), axis=0)
    used = jnp.any(flat[:, None] == block[None, :], axis=0).astype(jnp.int32)
    size = max(pairs, blocks)

    def row(values):
        return jnp.pad(values, (0, size - values.shape[0]))

    return jnp.stack(
        [
            row(order),
            row(order_block),
            row(again),
            row(jnp.maximum(upto - 1, 0)),
            row(used),
        ]
    )


def per_device_fused(
    tokens,
    routes,
    route_weight,
    base_index,
    expert_mask,
    base_gate,
    base_up,
    base_down,
    delta_in,
    delta_gate_up,
    delta_down_in,
    delta_out,
):
    rows, width = tokens.shape
    experts = lax.axis_size("exp")
    nz = experts // 4
    blocks = width // LANES
    count_blocks, per_block = base_index.shape
    pairs = count_blocks * per_block
    all_rows = rows * experts
    named = routes.T[:, None, :] == jnp.arange(experts, dtype=jnp.int32)[None, :, None]
    weights = jnp.sum(jnp.where(named, route_weight.T[:, None, :], 0.0), axis=0)
    weights = jnp.pad(
        jnp.concatenate([weights] * 3, axis=0), ((0, LANES - 3 * experts), (0, 0))
    ).T
    index_rows = base_index.T
    meta = tile_plan(index_rows, blocks)
    lift = delta_gate_up[0]
    units = lift.shape[2]
    bf16, f32 = jnp.bfloat16, jnp.float32
    vmem, smem, anywhere = (
        pl.BlockSpec(memory_space=space) for space in (pltpu.VMEM, pltpu.SMEM, pl.ANY)
    )
    dma = pltpu.SemaphoreType.DMA
    gather_cuts = 2
    reduce_cuts = 4 if blocks % 4 == 0 else 1
    return pl.pallas_call(
        functools.partial(fused_kernel, nz, gather_cuts, reduce_cuts),
        out_shape=jax.ShapeDtypeStruct((rows, width), bf16),
        in_specs=[vmem, vmem, smem, smem, smem] + [anywhere] * 7,
        out_specs=vmem,
        scratch_shapes=[
            pltpu.VMEM((all_rows, width + LANES), bf16),
            pltpu.VMEM((blocks, all_rows // 2, LANES), bf16),
            pltpu.VMEM((pairs, LANES, LANES), bf16),
            pltpu.VMEM((pairs, LANES, LANES), bf16),
            pltpu.VMEM((pairs, LANES, LANES), bf16),
            pltpu.VMEM((width, LANES), bf16),
            pltpu.VMEM((2, LANES, units), bf16),
            pltpu.VMEM((units, LANES), bf16),
            pltpu.VMEM((LANES, width), bf16),
            pltpu.VMEM((count_blocks, all_rows // 2, LANES), bf16),
            pltpu.VMEM((pairs, all_rows // 2, LANES), f32),
            pltpu.VMEM((all_rows, width), bf16),
            pltpu.VMEM((all_rows // 2, LANES), f32),
            pltpu.VMEM((nz, 2, rows, width), bf16),
            pltpu.VMEM((nz, rows, width), bf16),
            pltpu.VMEM((nz, rows, width), bf16),
            pltpu.VMEM((nz, rows, width), bf16),
            pltpu.VMEM((nz, rows, width), bf16),
            pltpu.VMEM((nz, rows, width), bf16),
            pltpu.VMEM((rows, width), f32),
            dma((7,)),
            dma((nz, gather_cuts)),
            dma((nz, gather_cuts)),
            dma((nz, 2, gather_cuts)),
            dma((nz, gather_cuts)),
            dma((nz, gather_cuts)),
            dma((nz, gather_cuts)),
            dma((nz, 2, gather_cuts)),
            dma((nz, 2)),
            dma((nz, reduce_cuts)),
            dma((nz, reduce_cuts)),
            dma((nz, reduce_cuts)),
            dma((nz, 2)),
            dma((nz, reduce_cuts)),
            dma((nz, reduce_cuts)),
        ],
        compiler_params=pltpu.CompilerParams(
            collective_id=0, has_side_effects=True, vmem_limit_bytes=60 << 20
        ),
        name="expert_layer",
    )(
        tokens,
        weights,
        index_rows,
        expert_mask[0].T,
        meta,
        base_gate.reshape(pairs, LANES, LANES),
        base_up.reshape(pairs, LANES, LANES),
        base_down.reshape(pairs, LANES, LANES),
        delta_in[0],
        lift,
        delta_down_in[0],
        delta_out[0],
    )


def place_rows(route_block, experts, most_rows, copies, copy_index):
    flat_routes = route_block.reshape(-1)
    onehot = (flat_routes[:, None] == jnp.arange(experts, dtype=jnp.int32)[None, :]).astype(
        jnp.int32
    )
    before = jnp.cumsum(onehot, axis=0) - onehot
    slot_index = jnp.sum(before * onehot, axis=1)
    return (flat_routes * copies + copy_index) * most_rows + slot_index


def spread_matrix(targets, slot_count, choose):
    matches = targets[None, :] == jnp.arange(slot_count, dtype=jnp.int32)[:, None]
    return jnp.any(matches.reshape(slot_count, -1, choose), axis=2).astype(jnp.bfloat16)


def hidden_units(incoming, index_part, keep_part, gate_tiles, up_tiles, delta_first, lift):
    row_count, model_width = incoming.shape
    blocks = model_width // 128
    count_blocks, per_block = index_part.shape
    picked = jnp.take(incoming.reshape(row_count, blocks, 128), index_part.reshape(-1), axis=1)
    picked = picked.reshape(row_count, count_blocks, per_block, 128)
    tile_keep = keep_part.astype(jnp.bfloat16)[:, :, None, None]
    pre_gate = jnp.einsum(
        "rfkc,fkch->rfh", picked, gate_tiles * tile_keep, preferred_element_type=jnp.float32
    ).reshape(row_count, -1)
    pre_up = jnp.einsum(
        "rfkc,fkch->rfh", picked, up_tiles * tile_keep, preferred_element_type=jnp.float32
    ).reshape(row_count, -1)
    lowrank = jnp.dot(incoming, delta_first, preferred_element_type=jnp.float32).astype(
        jnp.bfloat16
    )
    lifted = jnp.einsum("rq,gqh->grh", lowrank, lift, preferred_element_type=jnp.float32)
    return (jax.nn.silu(pre_gate + lifted[0]) * (pre_up + lifted[1])).astype(jnp.bfloat16)


def share_partial(hidden_part, index_part, keep_part, down_tiles, squeeze, delta_last):
    row_count = hidden_part.shape[0]
    count_blocks = down_tiles.shape[0]
    model_width = delta_last.shape[1]
    tile_keep = keep_part.astype(jnp.bfloat16)[:, :, None, None]
    pieces = jnp.einsum(
        "rfh,fkhc->rfkc",
        hidden_part.reshape(row_count, count_blocks, 128),
        down_tiles * tile_keep,
        preferred_element_type=jnp.float32,
    )
    placed = (
        jnp.zeros((row_count, model_width // 128, 128), jnp.float32)
        .at[:, index_part.reshape(-1)]
        .add(pieces.reshape(row_count, -1, 128))
    )
    squeezed = jnp.dot(hidden_part, squeeze, preferred_element_type=jnp.float32).astype(
        jnp.bfloat16
    )
    return placed.reshape(row_count, model_width) + jnp.dot(
        squeezed, delta_last, preferred_element_type=jnp.float32
    )


def per_device(
    tokens,
    routes,
    route_weight,
    base_index,
    expert_mask,
    base_gate,
    base_up,
    base_down,
    delta_in,
    delta_gate_up,
    delta_down_in,
    delta_out,
):
    tok_count, model_width = tokens.shape
    choose = routes.shape[1]
    exp_size = lax.axis_size("exp")
    base_size = lax.axis_size("base")
    half_blocks = base_gate.shape[0]
    most_rows = min(tok_count, max(2, (tok_count * choose + exp_size - 1) // exp_size * 3 // 2))
    own_targets = place_rows(routes, exp_size, most_rows, 1, 0)
    offset = lax.axis_index("base") * half_blocks
    my_index = lax.dynamic_slice_in_dim(base_index, offset, half_blocks, 0)
    my_keep = lax.dynamic_slice_in_dim(expert_mask[0], offset, half_blocks, 0)
    pair_tokens, pair_routes = (
        lax.all_gather(tokens, "base", axis=0, tiled=True),
        lax.all_gather(routes.astype(jnp.bfloat16), "base", axis=0, tiled=True),
    )
    pair_routes = pair_routes.astype(jnp.int32)
    targets = jnp.concatenate(
        [
            place_rows(
                pair_routes[copy_index * tok_count : (copy_index + 1) * tok_count],
                exp_size,
                most_rows,
                base_size,
                copy_index,
            )
            for copy_index in range(base_size)
        ]
    )
    spread = spread_matrix(targets, exp_size * base_size * most_rows, choose)
    outgoing = jnp.dot(spread, pair_tokens, preferred_element_type=jnp.float32).astype(jnp.bfloat16)
    outgoing = outgoing.reshape(exp_size, base_size * most_rows, model_width)
    arrived = lax.all_to_all(outgoing, "exp", split_axis=0, concat_axis=0, tiled=True)
    incoming = arrived.reshape(-1, model_width)
    hidden = hidden_units(
        incoming, my_index, my_keep, base_gate, base_up, delta_in[0], delta_gate_up[0]
    )
    partial_value = share_partial(
        hidden, my_index, my_keep, base_down, delta_down_in[0], delta_out[0]
    )
    summed = lax.psum_scatter(
        partial_value.reshape(exp_size, base_size, most_rows, model_width).astype(jnp.bfloat16),
        "base",
        scatter_dimension=1,
        tiled=True,
    )
    results = summed.reshape(exp_size, most_rows, model_width)
    returned = lax.all_to_all(results, "exp", split_axis=0, concat_axis=0, tiled=True).reshape(
        exp_size * most_rows, model_width
    )
    gathered = returned[own_targets.reshape(tok_count, choose)]
    combined = jnp.sum(route_weight[:, :, None] * gathered.astype(jnp.float32), axis=1)
    return combined.astype(jnp.bfloat16)


def solution(mesh):
    small = mesh.shape["base"] == 1 and mesh.shape["exp"] == 16
    return jax.shard_map(
        per_device_fused if small else per_device,
        mesh=mesh,
        in_specs=(
            P(("groups", "exp", "base"), None),
            P(("groups", "exp", "base"), None),
            P(("groups", "exp", "base"), None),
            P(),
            P("exp", None, None),
            P("base", None, None, None),
            P("base", None, None, None),
            P("base", None, None, None),
            P("exp", None, None),
            P("exp", None, None, "base"),
            P("exp", "base", None),
            P("exp", None, None),
        ),
        out_specs=P(("groups", "exp", "base"), None),
        check_vma=False,
    )
```

```python
import functools

import jax
import jax.numpy as jnp
from jax import lax
from jax.experimental import pallas as pl
from jax.experimental.pallas import tpu as pltpu
from jax.sharding import PartitionSpec as P

LANES = 128


def fused_kernel(
    nz,
    gather_cuts,
    reduce_cuts,
    tokens_ref,
    weight_ref,
    index_ref,
    keep_ref,
    meta_ref,
    gate_hbm,
    up_hbm,
    down_hbm,
    first_hbm,
    lift_hbm,
    squeeze_hbm,
    last_hbm,
    out_ref,
    tok,
    columns,
    gate_v,
    up_v,
    down_v,
    first_v,
    lift_v,
    squeeze_v,
    last_v,
    hidden,
    segment,
    part,
    scale,
    from_core,
    from_x,
    from_low,
    from_high,
    to_x,
    to_z,
    acc,
    weight_sem,
    gz_recv,
    gx_recv,
    gc_recv,
    gup_send,
    gdown_send,
    gx_send,
    gc_send,
    rc_recv,
    rx_recv,
    rlow_recv,
    rhigh_recv,
    rc_send,
    rx_send,
    rz_send,
):
    rows, width = tokens_ref.shape
    blocks = width // LANES
    pairs = gate_v.shape[0]
    count_blocks = hidden.shape[0]
    per_block = pairs // count_blocks
    all_rows = tok.shape[0]
    me = lax.axis_index("exp")
    core = lax.rem(me, 2)
    x = lax.rem(me // 2, 2)
    z = me // 4

    def place(pz, px, pc):
        return (pz * 2 + px) * 2 + pc

    core_peer = place(z, x, 1 - core)
    x_peer = place(z, 1 - x, core)
    up_peer = me + 4
    down_peer = me - 4
    has_up = z < nz - 1
    has_down = z > 0

    def fetch(position, source, target):
        return pltpu.make_async_copy(source, target, weight_sem.at[position])

    fetches = [
        fetch(0, first_hbm, first_v),
        fetch(1, gate_hbm, gate_v),
        fetch(2, up_hbm, up_v),
        fetch(3, lift_hbm, lift_v),
        fetch(4, down_hbm, down_v),
        fetch(5, squeeze_hbm, squeeze_v),
        fetch(6, last_hbm, last_v),
    ]

    barrier = pltpu.get_barrier_semaphore()

    def greet(peer):
        pl.semaphore_signal(
            barrier, inc=1, device_id={"exp": peer}, device_id_type=pl.DeviceIdType.MESH
        )

    greet(core_peer)
    greet(x_peer)

    @pl.when(has_up)
    def _():
        greet(up_peer)

    @pl.when(has_down)
    def _():
        greet(down_peer)

    own_rows = pl.ds(pl.multiple_of(me * rows, rows), rows)
    tok[own_rows, :width] = tokens_ref[...]
    weights = weight_ref[...]
    lane = lax.broadcasted_iota(jnp.int32, weights.shape, 1)
    high = weights.astype(jnp.bfloat16)
    rest = weights - high.astype(jnp.float32)
    middle = rest.astype(jnp.bfloat16)
    low_part = rest - middle.astype(jnp.float32)
    experts = 4 * nz
    tok[own_rows, width:] = jnp.where(
        lane < experts,
        high.astype(jnp.float32),
        jnp.where(lane < 2 * experts, middle.astype(jnp.float32), low_part),
    ).astype(jnp.bfloat16)

    degree = 2 + has_up.astype(jnp.int32) + has_down.astype(jnp.int32)
    pl.semaphore_wait(barrier, degree)

    def remote(source, target, send, recv, peer):
        return pltpu.make_async_remote_copy(
            src_ref=source,
            dst_ref=target,
            send_sem=send,
            recv_sem=recv,
            device_id={"exp": peer},
            device_id_type=pl.DeviceIdType.MESH,
        )

    all_blocks = blocks + 1
    edges = [(part * all_blocks // gather_cuts) * LANES for part in range(gather_cuts + 1)]
    gather_parts = range(gather_cuts)

    def block_of(pz, px, pc, cut):
        at = pl.ds(pl.multiple_of(place(pz, px, pc) * rows, rows), rows)
        return tok.at[at, pl.ds(edges[cut], edges[cut + 1] - edges[cut])]

    def g_up(pz, cut):
        b = block_of(pz, x, core, cut)
        return remote(b, b, gup_send.at[pz, cut], gz_recv.at[pz, cut], up_peer)

    def g_down(pz, cut):
        b = block_of(pz, x, core, cut)
        return remote(b, b, gdown_send.at[pz, cut], gz_recv.at[pz, cut], down_peer)

    def g_x(pz, px, cut):
        b = block_of(pz, px, core, cut)
        return remote(b, b, gx_send.at[pz, cut], gx_recv.at[pz, cut], x_peer)

    def g_core(pz, px, pc, cut):
        b = block_of(pz, px, pc, cut)
        return remote(b, b, gc_send.at[pz, px, cut], gc_recv.at[pz, px, cut], core_peer)

    def both_sides(distance, act):
        @pl.when(z >= distance)
        def _():
            act(z - distance, True)

        @pl.when(z + distance < nz)
        def _():
            act(z + distance, False)

    def spread_x(pz, cut):
        g_x(pz, x, cut).start()
        g_core(pz, x, core, cut).start()

    def pass_on(cut, pz, upward):
        if upward:
            g_up(pz, cut).wait_recv()

            @pl.when(has_up)
            def _():
                g_up(pz, cut).start()
        else:
            g_down(pz, cut).wait_recv()

            @pl.when(has_down)
            def _():
                g_down(pz, cut).start()
        spread_x(pz, cut)

    def cross(cut, pz, upward=True):
        g_x(pz, 1 - x, cut).wait_recv()
        g_core(pz, 1 - x, core, cut).start()

    def at_distance(distance, act, cut):
        if distance == 0:
            act(cut, z)
        else:
            both_sides(distance, functools.partial(act, cut))

    for cut in gather_parts:

        @pl.when(has_up)
        def _():
            g_up(z, cut).start()

        @pl.when(has_down)
        def _():
            g_down(z, cut).start()

        spread_x(z, cut)
    for one in fetches:
        one.start()
    half_rows = all_rows // 2
    own_half = z // (nz // 2)
    other_half = 1 - own_half

    def half_at(half):
        return pl.ds(pl.multiple_of(half * half_rows, half_rows), half_rows)

    def core_arrived(half):
        for step in range(nz // 2):
            for px in range(2):
                for cut in gather_parts:
                    g_core(half * (nz // 2) + step, px, 1 - core, cut).wait_recv()

    depth = 8 * LANES if blocks % 8 == 0 else LANES

    def keep_tile(value):
        some = jnp.full((16, LANES), value.astype(jnp.float32)).astype(jnp.bfloat16)
        return jnp.concatenate([some] * (LANES // 16), axis=0)

    def compute_hidden(half, meanwhile=None):
        at_rows = half_at(half)
        sent = tok[at_rows, width:].astype(jnp.float32)
        lane = lax.broadcasted_iota(jnp.int32, sent.shape, 1)
        mine = jnp.logical_and(lax.rem(lane, experts) == me, lane < 3 * experts)
        column = jnp.sum(jnp.where(mine, sent, 0.0), axis=1, keepdims=True)
        scale[...] = jnp.broadcast_to(column, scale.shape)

        def column_step(d, carry):
            columns[d] = tok[at_rows, pl.ds(pl.multiple_of(d * LANES, LANES), LANES)]
            return carry

        lax.fori_loop(0, blocks, column_step, 0, unroll=4)

        def low_step(step, total):
            at = pl.ds(pl.multiple_of(step * depth, depth), depth)
            return total + jnp.dot(
                tok[at_rows, at], first_v[at, :], preferred_element_type=jnp.float32
            )

        low = lax.fori_loop(
            0, width // depth, low_step, jnp.zeros((half_rows, LANES), jnp.float32)
        ).astype(jnp.bfloat16)

        if meanwhile is not None:
            meanwhile()

        def hidden_step(f, carry):
            left, right = [], []
            for k in range(per_block):
                pair = f * per_block + k
                left.append(columns[index_ref[k, f]])
                keep = keep_tile(keep_ref[k, f])
                right.append(jnp.concatenate([gate_v[pair] * keep, up_v[pair] * keep], axis=1))
            units = pl.ds(pl.multiple_of(f * LANES, LANES), LANES)
            left.append(low)
            right.append(jnp.concatenate([lift_v[0, :, units], lift_v[1, :, units]], axis=1))
            both = jnp.dot(
                jnp.concatenate(left, axis=1),
                jnp.concatenate(right, axis=0),
                preferred_element_type=jnp.float32,
            )
            gate, up = both[:, :LANES], both[:, LANES:]
            hidden[f] = (gate / (1.0 + jnp.exp(-gate)) * up).astype(jnp.bfloat16)
            return carry

        lax.fori_loop(0, count_blocks, hidden_step, 0, unroll=4)

    def compute_part(half):
        at_rows = half_at(half)

        def squeeze_step(f, total):
            at = pl.ds(pl.multiple_of(f * LANES, LANES), LANES)
            return total + jnp.dot(hidden[f], squeeze_v[at, :], preferred_element_type=jnp.float32)

        squeezed = lax.fori_loop(
            0, count_blocks, squeeze_step, jnp.zeros((half_rows, LANES), jnp.float32), unroll=8
        ).astype(jnp.bfloat16)

        def down_step(step, total):
            pair = meta_ref[0, step]
            f = meta_ref[1, step]
            tile = down_v[pair] * keep_tile(keep_ref[pair - f * per_block, f])
            again = meta_ref[2, step].astype(jnp.float32)
            total = total * again + jnp.dot(
                hidden[f], tile, preferred_element_type=jnp.float32
            )
            segment[step] = total
            return total

        lax.fori_loop(
            0, pairs, down_step, jnp.zeros((half_rows, LANES), jnp.float32), unroll=16
        )

        def output_step(d, carry):
            at = pl.ds(pl.multiple_of(d * LANES, LANES), LANES)
            value = jnp.dot(squeezed, last_v[:, at], preferred_element_type=jnp.float32)
            value = value + segment[meta_ref[3, d]] * meta_ref[4, d].astype(jnp.float32)
            value = value.astype(jnp.bfloat16).astype(jnp.float32) * scale[...]
            part[at_rows, at] = value.astype(jnp.bfloat16)
            return carry

        lax.fori_loop(0, blocks, output_step, 0, unroll=8)

    for distance in range(1, nz - 1):
        for cut in gather_parts:
            at_distance(distance, pass_on, cut)
            at_distance(distance - 1, cross, cut)
    core_arrived(own_half)
    for one in fetches[:4]:
        one.wait()

    compute_hidden(own_half)
    for cut in gather_parts:
        at_distance(nz - 1, pass_on, cut)
        at_distance(nz - 2, cross, cut)
    for one in fetches[4:]:
        one.wait()
    compute_part(own_half)
    for cut in gather_parts:
        at_distance(nz - 1, cross, cut)
    core_arrived(other_half)

    def part_of(pz, px, pc):
        return part.at[pl.ds(pl.multiple_of(place(pz, px, pc) * rows, rows), rows)]

    def r_core(pz, px):
        return remote(
            part_of(pz, px, 1 - core),
            from_core.at[pz, px],
            rc_send.at[pz, px],
            rc_recv.at[pz, px],
            core_peer,
        )

    step_width = width // reduce_cuts
    reduce_parts = range(reduce_cuts)

    def columns_of(cut):
        return pl.ds(cut * step_width, step_width)

    def r_x(pz, cut):
        at = columns_of(cut)
        return remote(
            to_x.at[pz, :, at],
            from_x.at[pz, :, at],
            rx_send.at[pz, cut],
            rx_recv.at[pz, cut],
            x_peer,
        )

    def r_up(pz, cut):
        at = columns_of(cut)
        return remote(
            to_z.at[pz, :, at],
            from_low.at[pz, :, at],
            rz_send.at[pz, cut],
            rlow_recv.at[pz, cut],
            up_peer,
        )

    def r_down(pz, cut):
        at = columns_of(cut)
        return remote(
            to_z.at[pz, :, at],
            from_high.at[pz, :, at],
            rz_send.at[pz, cut],
            rhigh_recv.at[pz, cut],
            down_peer,
        )

    def wide(value):
        return value.astype(jnp.float32)

    def core_start(pz, px):
        r_core(pz, px).start()

    mate = own_half * nz + nz // 2 - 1 - z
    toward = 1 - 2 * own_half
    near = jnp.where(own_half == 0, nz // 2, nz // 2 - 1)
    far = near + toward * (nz // 2 - 1)
    at_end = jnp.logical_or(z == 0, z == nz - 1)

    def part_at(pz, px, cut):
        at = pl.ds(pl.multiple_of(place(pz, px, core) * rows, rows), rows)
        return wide(part[at, columns_of(cut)])

    def x_start(pz):
        r_core(pz, 1 - x).wait_recv()
        for cut in reduce_parts:
            at = columns_of(cut)
            total = part_at(pz, 1 - x, cut) + wide(from_core[pz, 1 - x, :, at])
            to_x[pz, :, at] = total.astype(jnp.bfloat16)
            r_x(pz, cut).start()

    def local_sum(pz, cut):
        r_x(pz, cut).wait_recv()
        at = columns_of(cut)
        total = part_at(pz, x, cut) + wide(from_core[pz, x, :, at])
        return total + wide(from_x[pz, :, at])

    def z_step(pz):
        r_core(pz, x).wait_recv()
        for cut in reduce_parts:
            at = columns_of(cut)
            acc[:, at] = local_sum(pz, cut)

            @pl.when(pz < z)
            def _():
                @pl.when(has_up)
                def _():
                    r_down(pz, cut).wait_recv()
                    acc[:, at] += wide(from_high[pz, :, at])

                to_z[pz, :, at] = acc[:, at].astype(jnp.bfloat16)
                r_down(pz, cut).start()

            @pl.when(pz > z)
            def _():
                @pl.when(has_down)
                def _():
                    r_up(pz, cut).wait_recv()
                    acc[:, at] += wide(from_low[pz, :, at])

                to_z[pz, :, at] = acc[:, at].astype(jnp.bfloat16)
                r_up(pz, cut).start()

    for px in (1 - x, x):
        core_start(mate, px)
        core_start(z, px)

    def near_sums():
        x_start(mate)
        x_start(z)

    compute_hidden(other_half, near_sums)
    compute_part(other_half)
    for px in (1 - x, x):
        core_start(far, px)
        core_start(near, px)

    x_start(far)
    x_start(near)

    @pl.when(at_end)
    def _():
        z_step(mate)

    z_step(far)

    @pl.when(jnp.logical_not(at_end))
    def _():
        z_step(mate)

    z_step(near)
    r_core(z, x).wait_recv()
    for cut in reduce_parts:
        at = columns_of(cut)
        acc[:, at] = local_sum(z, cut)

        @pl.when(has_up)
        def _():
            r_down(z, cut).wait_recv()
            acc[:, at] += wide(from_high[z, :, at])

        @pl.when(has_down)
        def _():
            r_up(z, cut).wait_recv()
            acc[:, at] += wide(from_low[z, :, at])

        out_ref[:, at] = acc[:, at].astype(jnp.bfloat16)

    for pz in range(nz):
        for px in range(2):
            r_core(pz, px).wait_send()
        for cut in reduce_parts:
            r_x(pz, cut).wait_send()

            @pl.when(pz != z)
            def _():
                r_up(pz, cut).wait_send()

    for pz in range(nz):
        for cut in gather_parts:

            @pl.when(jnp.logical_and(has_up, pz <= z))
            def _():
                g_up(pz, cut).wait_send()

            @pl.when(jnp.logical_and(has_down, pz >= z))
            def _():
                g_down(pz, cut).wait_send()

            g_x(pz, x, cut).wait_send()
            for px in range(2):
                g_core(pz, px, core, cut).wait_send()


def tile_plan(index_rows, blocks):
    per_block, count_blocks = index_rows.shape
    flat = index_rows.reshape(-1)
    pairs = flat.shape[0]
    place = jnp.arange(pairs, dtype=jnp.int32)
    ahead = (flat[:, None] < flat[None, :]) | (
        (flat[:, None] == flat[None, :]) & (place[:, None] < place[None, :])
    )
    rank = jnp.sum(ahead.astype(jnp.int32), axis=0)
    chosen = (rank[:, None] == place[None, :]).astype(jnp.int32)
    unit_block = place % count_blocks
    stored = unit_block * per_block + place // count_blocks
    order = jnp.sum(chosen * stored[:, None], axis=0)
    order_block = jnp.sum(chosen * unit_block[:, None], axis=0)
    sorted_block = jnp.sum(chosen * flat[:, None], axis=0)
    again = jnp.concatenate(
        [jnp.zeros((1,), jnp.int32), (sorted_block[1:] == sorted_block[:-1]).astype(jnp.int32)]
    )
    block = jnp.arange(blocks, dtype=jnp.int32)
    upto = jnp.sum((flat[:, None] <= block[None, :]).astype(jnp.int32), axis=0)
    used = jnp.any(flat[:, None] == block[None, :], axis=0).astype(jnp.int32)
    size = max(pairs, blocks)

    def row(values):
        return jnp.pad(values, (0, size - values.shape[0]))

    return jnp.stack(
        [
            row(order),
            row(order_block),
            row(again),
            row(jnp.maximum(upto - 1, 0)),
            row(used),
        ]
    )


def per_device_fused(
    tokens,
    routes,
    route_weight,
    base_index,
    expert_mask,
    base_gate,
    base_up,
    base_down,
    delta_in,
    delta_gate_up,
    delta_down_in,
    delta_out,
):
    rows, width = tokens.shape
    experts = lax.axis_size("exp")
    nz = experts // 4
    blocks = width // LANES
    count_blocks, per_block = base_index.shape
    pairs = count_blocks * per_block
    all_rows = rows * experts
    named = routes.T[:, None, :] == jnp.arange(experts, dtype=jnp.int32)[None, :, None]
    weights = jnp.sum(jnp.where(named, route_weight.T[:, None, :], 0.0), axis=0)
    weights = jnp.pad(
        jnp.concatenate([weights] * 3, axis=0), ((0, LANES - 3 * experts), (0, 0))
    ).T
    index_rows = base_index.T
    meta = tile_plan(index_rows, blocks)
    lift = delta_gate_up[0]
    units = lift.shape[2]
    bf16, f32 = jnp.bfloat16, jnp.float32
    vmem, smem, anywhere = (
        pl.BlockSpec(memory_space=space) for space in (pltpu.VMEM, pltpu.SMEM, pl.ANY)
    )
    dma = pltpu.SemaphoreType.DMA
    gather_cuts = 2
    reduce_cuts = 4 if blocks % 4 == 0 else 1
    return pl.pallas_call(
        functools.partial(fused_kernel, nz, gather_cuts, reduce_cuts),
        out_shape=jax.ShapeDtypeStruct((rows, width), bf16),
        in_specs=[vmem, vmem, smem, smem, smem] + [anywhere] * 7,
        out_specs=vmem,
        scratch_shapes=[
            pltpu.VMEM((all_rows, width + LANES), bf16),
            pltpu.VMEM((blocks, all_rows // 2, LANES), bf16),
            pltpu.VMEM((pairs, LANES, LANES), bf16),
            pltpu.VMEM((pairs, LANES, LANES), bf16),
            pltpu.VMEM((pairs, LANES, LANES), bf16),
            pltpu.VMEM((width, LANES), bf16),
            pltpu.VMEM((2, LANES, units), bf16),
            pltpu.VMEM((units, LANES), bf16),
            pltpu.VMEM((LANES, width), bf16),
            pltpu.VMEM((count_blocks, all_rows // 2, LANES), bf16),
            pltpu.VMEM((pairs, all_rows // 2, LANES), f32),
            pltpu.VMEM((all_rows, width), bf16),
            pltpu.VMEM((all_rows // 2, LANES), f32),
            pltpu.VMEM((nz, 2, rows, width), bf16),
            pltpu.VMEM((nz, rows, width), bf16),
            pltpu.VMEM((nz, rows, width), bf16),
            pltpu.VMEM((nz, rows, width), bf16),
            pltpu.VMEM((nz, rows, width), bf16),
            pltpu.VMEM((nz, rows, width), bf16),
            pltpu.VMEM((rows, width), f32),
            dma((7,)),
            dma((nz, gather_cuts)),
            dma((nz, gather_cuts)),
            dma((nz, 2, gather_cuts)),
            dma((nz, gather_cuts)),
            dma((nz, gather_cuts)),
            dma((nz, gather_cuts)),
            dma((nz, 2, gather_cuts)),
            dma((nz, 2)),
            dma((nz, reduce_cuts)),
            dma((nz, reduce_cuts)),
            dma((nz, reduce_cuts)),
            dma((nz, 2)),
            dma((nz, reduce_cuts)),
            dma((nz, reduce_cuts)),
        ],
        compiler_params=pltpu.CompilerParams(
            collective_id=0, has_side_effects=True, vmem_limit_bytes=60 << 20
        ),
        name="expert_layer",
    )(
        tokens,
        weights,
        index_rows,
        expert_mask[0].T,
        meta,
        base_gate.reshape(pairs, LANES, LANES),
        base_up.reshape(pairs, LANES, LANES),
        base_down.reshape(pairs, LANES, LANES),
        delta_in[0],
        lift,
        delta_down_in[0],
        delta_out[0],
    )


def place_rows(route_block, experts, most_rows, copies, copy_index):
    flat_routes = route_block.reshape(-1)
    onehot = (flat_routes[:, None] == jnp.arange(experts, dtype=jnp.int32)[None, :]).astype(
        jnp.int32
    )
    before = jnp.cumsum(onehot, axis=0) - onehot
    slot_index = jnp.sum(before * onehot, axis=1)
    return (flat_routes * copies + copy_index) * most_rows + slot_index


def spread_matrix(targets, slot_count, choose):
    matches = targets[None, :] == jnp.arange(slot_count, dtype=jnp.int32)[:, None]
    return jnp.any(matches.reshape(slot_count, -1, choose), axis=2).astype(jnp.bfloat16)


def hidden_units(incoming, index_part, keep_part, gate_tiles, up_tiles, delta_first, lift):
    row_count, model_width = incoming.shape
    blocks = model_width // 128
    count_blocks, per_block = index_part.shape
    picked = jnp.take(incoming.reshape(row_count, blocks, 128), index_part.reshape(-1), axis=1)
    picked = picked.reshape(row_count, count_blocks, per_block, 128)
    tile_keep = keep_part.astype(jnp.bfloat16)[:, :, None, None]
    pre_gate = jnp.einsum(
        "rfkc,fkch->rfh", picked, gate_tiles * tile_keep, preferred_element_type=jnp.float32
    ).reshape(row_count, -1)
    pre_up = jnp.einsum(
        "rfkc,fkch->rfh", picked, up_tiles * tile_keep, preferred_element_type=jnp.float32
    ).reshape(row_count, -1)
    lowrank = jnp.dot(incoming, delta_first, preferred_element_type=jnp.float32).astype(
        jnp.bfloat16
    )
    lifted = jnp.einsum("rq,gqh->grh", lowrank, lift, preferred_element_type=jnp.float32)
    return (jax.nn.silu(pre_gate + lifted[0]) * (pre_up + lifted[1])).astype(jnp.bfloat16)


def share_partial(hidden_part, index_part, keep_part, down_tiles, squeeze, delta_last):
    row_count = hidden_part.shape[0]
    count_blocks = down_tiles.shape[0]
    model_width = delta_last.shape[1]
    tile_keep = keep_part.astype(jnp.bfloat16)[:, :, None, None]
    pieces = jnp.einsum(
        "rfh,fkhc->rfkc",
        hidden_part.reshape(row_count, count_blocks, 128),
        down_tiles * tile_keep,
        preferred_element_type=jnp.float32,
    )
    placed = (
        jnp.zeros((row_count, model_width // 128, 128), jnp.float32)
        .at[:, index_part.reshape(-1)]
        .add(pieces.reshape(row_count, -1, 128))
    )
    squeezed = jnp.dot(hidden_part, squeeze, preferred_element_type=jnp.float32).astype(
        jnp.bfloat16
    )
    return placed.reshape(row_count, model_width) + jnp.dot(
        squeezed, delta_last, preferred_element_type=jnp.float32
    )


def per_device(
    tokens,
    routes,
    route_weight,
    base_index,
    expert_mask,
    base_gate,
    base_up,
    base_down,
    delta_in,
    delta_gate_up,
    delta_down_in,
    delta_out,
):
    tok_count, model_width = tokens.shape
    choose = routes.shape[1]
    exp_size = lax.axis_size("exp")
    base_size = lax.axis_size("base")
    half_blocks = base_gate.shape[0]
    most_rows = min(tok_count, max(2, (tok_count * choose + exp_size - 1) // exp_size * 3 // 2))
    own_targets = place_rows(routes, exp_size, most_rows, 1, 0)
    offset = lax.axis_index("base") * half_blocks
    my_index = lax.dynamic_slice_in_dim(base_index, offset, half_blocks, 0)
    my_keep = lax.dynamic_slice_in_dim(expert_mask[0], offset, half_blocks, 0)
    pair_tokens, pair_routes = (
        lax.all_gather(tokens, "base", axis=0, tiled=True),
        lax.all_gather(routes.astype(jnp.bfloat16), "base", axis=0, tiled=True),
    )
    pair_routes = pair_routes.astype(jnp.int32)
    targets = jnp.concatenate(
        [
            place_rows(
                pair_routes[copy_index * tok_count : (copy_index + 1) * tok_count],
                exp_size,
                most_rows,
                base_size,
                copy_index,
            )
            for copy_index in range(base_size)
        ]
    )
    spread = spread_matrix(targets, exp_size * base_size * most_rows, choose)
    outgoing = jnp.dot(spread, pair_tokens, preferred_element_type=jnp.float32).astype(jnp.bfloat16)
    outgoing = outgoing.reshape(exp_size, base_size * most_rows, model_width)
    arrived = lax.all_to_all(outgoing, "exp", split_axis=0, concat_axis=0, tiled=True)
    incoming = arrived.reshape(-1, model_width)
    hidden = hidden_units(
        incoming, my_index, my_keep, base_gate, base_up, delta_in[0], delta_gate_up[0]
    )
    partial_value = share_partial(
        hidden, my_index, my_keep, base_down, delta_down_in[0], delta_out[0]
    )
    summed = lax.psum_scatter(
        partial_value.reshape(exp_size, base_size, most_rows, model_width).astype(jnp.bfloat16),
        "base",
        scatter_dimension=1,
        tiled=True,
    )
    results = summed.reshape(exp_size, most_rows, model_width)
    returned = lax.all_to_all(results, "exp", split_axis=0, concat_axis=0, tiled=True).reshape(
        exp_size * most_rows, model_width
    )
    gathered = returned[own_targets.reshape(tok_count, choose)]
    combined = jnp.sum(route_weight[:, :, None] * gathered.astype(jnp.float32), axis=1)
    return combined.astype(jnp.bfloat16)


def solution(mesh):
    small = mesh.shape["base"] == 1 and mesh.shape["exp"] == 16
    return jax.shard_map(
        per_device_fused if small else per_device,
        mesh=mesh,
        in_specs=(
            P(("groups", "exp", "base"), None),
            P(("groups", "exp", "base"), None),
            P(("groups", "exp", "base"), None),
            P(),
            P("exp", None, None),
            P("base", None, None, None),
            P("base", None, None, None),
            P("base", None, None, None),
            P("exp", None, None),
            P("exp", None, None, "base"),
            P("exp", "base", None),
            P("exp", None, None),
        ),
        out_specs=P(("groups", "exp", "base"), None),
        check_vma=False,
    )
```
